256 devices in a mesh: dp: 32 (over x, z), mp: 8 (over y, core).
Axes of the slice: x: 4, y: 4, z: 8, core: 2. Of those that a mesh axis runs over, the one named last changes fastest.
Arguments:
- teacher_feat: bfloat16 [3072, 256], P('dp'), may hold values from -6 to 6
- student_feat: bfloat16 [15360, 256], P('dp'), may hold values from -6 to 6
- teacher_weight: bfloat16 [256, 65536], P(None, 'mp'), may hold values from -1.5 to 1.5
- student_weight: bfloat16 [256, 65536], P(None, 'mp'), may hold values from -0.375 to 0.375
- crop_to_image: int32 [15360], P('dp'), may hold values from 0 to 95
Outputs:
- feat_grad: float32 [15360, 256], P('dp', 'mp')
- proto_grad: float32 [256, 65536], P('dp', 'mp')
The draws below stay inside these ranges and needn't reach their ends.
Inputs may be any that keep to these rules, and one draw needn't show every extreme that they name: `crop_to_image`: crop c of the data block d names teacher row d * 96 + crop_to_image_c.
All inputs are finite; a program needn't handle non-finite values.
Results may differ from the reference program's by a relative error of at most 0.0015.
The reference program's roundings to bfloat16 on the way (of `teacher_norm`, `student_norm` and `dlog`) count: a program that leaves them out, or rounds other values in their place, can miss the bound.
Values sent between devices are 32-bit elements; how exact they have to be, the bound alone decides.
No kernel may reach another device: no remote copies, remote signals or barrier semaphores. Data moves between devices by JAX's collectives and lax.ppermute only.
A program may use at most 128 MiB of HBM per device.

```python
import jax
import jax.numpy as jnp
from jax import lax

K = 256
P_SIZE = 65536
TB_DEV = 96
ITERS = 3
SB_DEV = 480
TB_TOTAL = 3072
SB_TOTAL = 15360
N_DP = 32


def shared_centres(key):
    return jax.random.normal(jax.random.fold_in(key, 11), (16, K), jnp.float32)


def draw_teacher_feat(key, part):
    clusters = 16
    centres = shared_centres(key)
    first_pick = jax.random.randint(jax.random.fold_in(key, 21), (TB_TOTAL,), 0, clusters)
    second_pick = jax.random.randint(jax.random.fold_in(key, 22), (TB_TOTAL,), 0, clusters)
    cluster_id = jnp.minimum(first_pick, second_pick)
    anchor = jnp.take(centres, cluster_id, axis=0)
    jitter = jax.random.normal(jax.random.fold_in(key, 23), (TB_TOTAL, K), jnp.float32)
    values = anchor + jitter
    return jnp.clip(values, -6.0, 6.0).astype(jnp.bfloat16)


def draw_teacher_weight(key, part):
    clusters = 16
    centres = shared_centres(key)
    block_width = max(P_SIZE // 256, 1)
    block_count = P_SIZE // block_width
    block_owner = jax.random.randint(jax.random.fold_in(key, 31), (block_count,), 0, clusters + clusters // 2)
    column_owner = jnp.repeat(block_owner, block_width)
    aligned = (column_owner < clusters).astype(jnp.float32)
    anchor = jnp.take(centres, jnp.minimum(column_owner, clusters - 1), axis=0) * aligned[:, None]
    anchor = anchor.T
    factor = 0.70710678 * K ** (-0.5)
    jitter = jax.random.normal(jax.random.fold_in(key, 32), (K, P_SIZE), jnp.float32)
    values = (anchor + jitter) * factor
    return jnp.clip(values, -1.5, 1.5).astype(jnp.bfloat16)


def set_ends(entries, stream_key, smallest, top_value):
    dims = entries.shape
    index_at = [jax.random.randint(jax.random.fold_in(stream_key, axis), (), 0, dims[axis]) for axis in range(len(dims))]
    entries = entries.at[tuple(index_at)].set(smallest)
    longest = dims.index(max(dims))
    index_at[longest] = (index_at[longest] + 1) % dims[longest]
    return entries.at[tuple(index_at)].set(top_value)


def steps_of(own_key, dims, pieces, least, top_value):
    loudness = 1.0
    for position, blocks in pieces:
        draws = jax.random.uniform(jax.random.fold_in(jax.random.fold_in(own_key, 6), position), (blocks,), jnp.float32, least / len(pieces), top_value / len(pieces))
        loudness = loudness * jnp.repeat(jnp.exp(draws), dims[position] // blocks).reshape((-1,) + (1,) * (len(dims) - 1 - position))
    return loudness


def noise(stream_key, shape, width, reach, cuts=(), dtype=jnp.bfloat16):
    values = jax.random.normal(stream_key, shape, jnp.float32) * width
    if len(cuts) > 0:
        values = steps_of(stream_key, shape, cuts, -0.22, 0.18) * values
    return jnp.clip(values, min=-reach, max=reach).astype(dtype)


def setup_inputs(seed: int = 0) -> dict:
    splits = jax.random.split(jax.random.key(seed), 6)
    return {
        "teacher_feat": draw_teacher_feat(jax.random.fold_in(splits[5], 71), 0),
        "student_feat": noise(splits[1], (SB_TOTAL, K), 1.0, 6.0, ((0, 32),)),
        "teacher_weight": draw_teacher_weight(jax.random.fold_in(splits[5], 71), 0),
        "student_weight": noise(splits[3], (K, P_SIZE), K ** -0.5, 0.375, ((1, 8),)),
        "crop_to_image": set_ends(jax.random.randint(splits[4], (SB_TOTAL,), 0, TB_DEV), jax.random.fold_in(splits[4], 1), 0, TB_DEV - 1).astype(jnp.int32),
    }


eps = 1e-06
t_temp = 0.07
s_temp = 0.1
loss_scale = 1024.0

def row_unit(x):
    values = x.astype(jnp.float32)
    inverse = lax.rsqrt(lax.optimization_barrier(jnp.sum(values * values, axis=1, keepdims=True)) + eps)
    return (values * inverse, inverse)

def col_unit(w):
    values = w.astype(jnp.float32)
    return (values * lax.rsqrt(lax.optimization_barrier(jnp.sum(values * values, axis=0, keepdims=True)) + eps)).astype(jnp.bfloat16)

def reference(teacher_feat, student_feat, teacher_weight, student_weight, crop_to_image):
    teacher_unit, _ = row_unit(teacher_feat)
    teacher_norm = col_unit(teacher_weight)
    scores = jnp.dot(teacher_unit.astype(jnp.bfloat16), teacher_norm, preferred_element_type=jnp.float32)
    q = jnp.exp(scores / t_temp)
    for step in range(ITERS):
        column = lax.optimization_barrier(jnp.sum(q, axis=0, keepdims=True))
        q = q / (column * P_SIZE)
        row_total = lax.optimization_barrier(jnp.sum(q, axis=1, keepdims=True))
        q = q / (row_total * TB_TOTAL)
    targets = q * TB_TOTAL
    student_norm = col_unit(student_weight)
    target_blocks = targets.reshape(N_DP, TB_DEV, P_SIZE)
    feat_blocks = student_feat.reshape(N_DP, SB_DEV, K)
    index_blocks = crop_to_image.reshape(N_DP, SB_DEV)

    def block_step(carry, inputs):
        target_block, feat_block, index_block = inputs
        unit_rows, inverse = row_unit(feat_block)
        unit_bf = unit_rows.astype(jnp.bfloat16)
        logits = jnp.dot(unit_bf, student_norm, preferred_element_type=jnp.float32) / s_temp
        expo = jnp.exp(logits)
        probs = expo / lax.optimization_barrier(jnp.sum(expo, axis=1, keepdims=True))
        picked = jnp.take(target_block, index_block.astype(jnp.int32), axis=0)
        dlog = (loss_scale * (probs - picked) / s_temp).astype(jnp.bfloat16)
        grad_rows = lax.dot_general(dlog, student_norm, (((1,), (1,)), ((), ())), preferred_element_type=jnp.float32)
        feat_part = (grad_rows - unit_rows * lax.optimization_barrier(jnp.sum(unit_rows * grad_rows, axis=1, keepdims=True))) * inverse
        carry = carry + lax.dot_general(unit_bf, dlog, (((0,), (0,)), ((), ())), preferred_element_type=jnp.float32)
        return (carry, feat_part)
    proto_grad, feat_parts = lax.scan(block_step, jnp.zeros((K, P_SIZE), jnp.float32), (target_blocks, feat_blocks, index_blocks))
    return (feat_parts.reshape(SB_TOTAL, K), proto_grad)
```

```python
import functools

import jax
import jax.numpy as jnp
from jax import lax
from jax.experimental import pallas as pl
from jax.experimental.pallas import tpu as pltpu
from jax.sharding import Mesh
from jax.sharding import PartitionSpec as P

K = 256
P_SIZE = 65536
TB_DEV = 96
TB_TOTAL = 3072
ITERS = 3
SB_DEV = 480
NX, NZ, NY, NC = 4, 8, 4, 2
NROW = NX * NY * NC
COLS = P_SIZE // NROW
LG = COLS // 128
TROWS = NX * TB_DEV
SROWS = NX * SB_DEV
BLK = 512
NB = COLS // BLK

eps = 1e-06
t_temp = 0.07
s_temp = 0.1
loss_scale = 1024.0

f32 = jnp.float32
bf16 = jnp.bfloat16
VMEM_LIMIT = 56 * 1024 * 1024


def unit_scale(v):
    return lax.rsqrt(jnp.sum(v * v, axis=1, keepdims=True) + eps)


def norm_columns(w):
    v = w.astype(f32)
    return (v * lax.rsqrt(jnp.sum(v * v, axis=0, keepdims=True) + eps)).astype(bf16)


def dot(a, b, ca, cb):
    return lax.dot_general(a, b, (((ca,), (cb,)), ((), ())), preferred_element_type=f32)


def lane_groups(v):
    return jnp.concatenate([v[:, 128 * k : 128 * (k + 1)] for k in range(v.shape[1] // 128)], 0)


def teacher_kernel(ix, tf, tw, e_out, c_out, tn_out, tu_out):
    j = pl.program_id(0)

    @pl.when(j == 0)
    def _():
        for x in range(NX):
            v = tf[x, :TB_DEV, :]
            tu_out[x * TB_DEV : (x + 1) * TB_DEV, :] = (v * unit_scale(v)).astype(bf16)

    tn = norm_columns(tw[...])
    tn_out[...] = tn
    e = jnp.exp(dot(tu_out[...], tn, 1, 0) * (1.0 / t_temp))
    e_out[...] = e
    col = lane_groups(jnp.sum(e, axis=0, keepdims=True))
    c_out[...] = jnp.broadcast_to(col[None], c_out.shape)


def teacher_pass(ix, tf_all, tw):
    return pl.pallas_call(
        teacher_kernel,
        grid_spec=pltpu.PrefetchScalarGridSpec(
            num_scalar_prefetch=1,
            grid=(2,),
            in_specs=[
                pl.BlockSpec((NX, TB_DEV + 8, K), lambda j, ix: (0, 0, 0)),
                pl.BlockSpec((K, 1024), lambda j, ix: (0, ix[0] * 2 + j)),
            ],
            out_specs=[
                pl.BlockSpec((TROWS, 1024), lambda j, ix: (0, j)),
                pl.BlockSpec((NZ, 8, 128), lambda j, ix: (0, j, 0)),
                pl.BlockSpec((K, 1024), lambda j, ix: (0, j)),
                pl.BlockSpec((TROWS, K), lambda j, ix: (0, 0)),
            ],
        ),
        out_shape=[
            jax.ShapeDtypeStruct((TROWS, COLS), f32),
            jax.ShapeDtypeStruct((NZ, LG, 128), f32),
            jax.ShapeDtypeStruct((K, COLS), bf16),
            jax.ShapeDtypeStruct((TROWS, K), bf16),
        ],
        compiler_params=pltpu.CompilerParams(vmem_limit_bytes=VMEM_LIMIT),
        name="teacher_scores",
    )(ix, tf_all, tw)


def student_kernel(ix, sf, ci, tu, sw, ub_out, tuc_out, sn_out, rs_out, acc):
    j = pl.program_id(0)

    @pl.when(j == 0)
    def _():
        for x in range(NX):
            rows = slice(x * SB_DEV, (x + 1) * SB_DEV)
            v = sf[x]
            ub_out[rows, :] = (v * unit_scale(v)).astype(bf16)
            pick = lax.broadcasted_iota(jnp.int32, (SB_DEV, TB_DEV), 1) == ci[rows, :]
            pick = jnp.where(pick, 1.0, 0.0).astype(bf16)
            tuc_out[rows, :] = dot(
                pick, tu[x * TB_DEV : (x + 1) * TB_DEV, :], 1, 0
            ).astype(bf16)
        acc[...] = jnp.zeros_like(acc)

    sn = norm_columns(sw[...])
    sn_out[...] = sn
    for x in range(NX):
        rows = slice(x * SB_DEV, (x + 1) * SB_DEV)
        e = jnp.exp(dot(ub_out[rows, :], sn, 1, 0) * (1.0 / s_temp))
        total = e[:, :128]
        for k in range(1, BLK // 128):
            total = total + e[:, 128 * k : 128 * (k + 1)]
        acc[rows, :] += total

    @pl.when(j == NB - 1)
    def _():
        for k in range(SROWS // 128):
            rows = slice(128 * k, 128 * (k + 1))
            rs_out[k : k + 1, :] = jnp.sum(acc[rows, :].T, axis=0, keepdims=True)
        rs_out[SROWS // 128 :, :] = jnp.zeros((1, 128), f32)


def student_pass(ix, sf_all, ci, tu, sw):
    whole = lambda shape: pl.BlockSpec(shape, lambda j, ix: (0,) * len(shape))
    return pl.pallas_call(
        student_kernel,
        grid_spec=pltpu.PrefetchScalarGridSpec(
            num_scalar_prefetch=1,
            grid=(NB,),
            in_specs=[
                whole((NX, SB_DEV, K)),
                whole((SROWS, 1)),
                whole((TROWS, K)),
                pl.BlockSpec((K, BLK), lambda j, ix: (0, ix[0] * NB + j)),
            ],
            out_specs=[
                whole((SROWS, K)),
                whole((SROWS, K)),
                pl.BlockSpec((K, BLK), lambda j, ix: (0, j)),
                whole((16, 128)),
            ],
            scratch_shapes=[pltpu.VMEM((SROWS, 128), f32)],
        ),
        out_shape=[
            jax.ShapeDtypeStruct((SROWS, K), bf16),
            jax.ShapeDtypeStruct((SROWS, K), bf16),
            jax.ShapeDtypeStruct((K, COLS), bf16),
            jax.ShapeDtypeStruct((16, 128), f32),
        ],
        compiler_params=pltpu.CompilerParams(vmem_limit_bytes=VMEM_LIMIT),
        name="student_sums",
    )(ix, sf_all, ci, tu, sw)


def row_kernel(c_parts, e, b_out, r_out):
    b = 1.0 / (jnp.sum(c_parts[...], axis=0) * P_SIZE)
    b_out[...] = b
    acc = e[:, :128] * b[0:1, :]
    for k in range(1, LG):
        acc = acc + e[:, 128 * k : 128 * (k + 1)] * b[k : k + 1, :]
    for k in range(TROWS // 128):
        r = jnp.sum(acc[128 * k : 128 * (k + 1), :].T, axis=0, keepdims=True)
        r_out[:, k : k + 1, :] = jnp.broadcast_to(r[None], (NROW, 1, 128))
    r_out[:, TROWS // 128 :, :] = jnp.zeros((NROW, 8 - TROWS // 128, 128), f32)


def row_pass(c_parts, e):
    return pl.pallas_call(
        row_kernel,
        out_shape=[
            jax.ShapeDtypeStruct((LG, 128), f32),
            jax.ShapeDtypeStruct((NROW, 8, 128), f32),
        ],
        compiler_params=pltpu.CompilerParams(vmem_limit_bytes=VMEM_LIMIT),
        name="row_sums",
    )(c_parts, e)


def col_kernel(r_parts, e, c_out):
    a = 1.0 / (jnp.sum(r_parts[...], axis=0)[:3] * TB_TOTAL)
    wide = jnp.concatenate(
        [jnp.broadcast_to(a[k : k + 1, :], (128, 128)).T for k in range(TROWS // 128)], 0
    )
    for k in range(LG):
        c = jnp.sum(e[:, 128 * k : 128 * (k + 1)] * wide, axis=0, keepdims=True)
        c_out[:, k : k + 1, :] = jnp.broadcast_to(c[None], (NZ, 1, 128))


def col_pass(r_parts, e):
    return pl.pallas_call(
        col_kernel,
        out_shape=jax.ShapeDtypeStruct((NZ, LG, 128), f32),
        compiler_params=pltpu.CompilerParams(vmem_limit_bytes=VMEM_LIMIT),
        name="col_sums",
    )(r_parts, e)


def grad_kernel(ub, tuc, ci, rt, st, b, sn, tn, p_out, g0_out, g1_out, g, coef):
    j = pl.program_id(0)

    @pl.when(j == 0)
    def _():
        lane = lax.broadcasted_iota(jnp.int32, (SB_DEV, TB_DEV), 1)
        for x in range(NX):
            rows = slice(x * SB_DEV, (x + 1) * SB_DEV)
            a = (loss_scale / s_temp) / rt[x : x + 1, :]
            pick = jnp.where(lane == ci[rows, :], jnp.broadcast_to(a, (SB_DEV, TB_DEV)), 0.0)
            coef[rows, 0:1] = jnp.sum(pick, axis=1, keepdims=True)
        for k in range(SROWS // 128):
            rows = slice(128 * k, 128 * (k + 1))
            s = (loss_scale / s_temp) / st[k : k + 1, :]
            coef[rows, 1:2] = jnp.broadcast_to(s, (128, 128)).T[:, 0:1]

    for x in range(NX):
        rows = slice(x * SB_DEV, (x + 1) * SB_DEV)
        p = jnp.exp(dot(ub[rows, :], sn[...], 1, 0) * (1.0 / s_temp)) * coef[rows, 1:2]
        t = jnp.exp(dot(tuc[rows, :], tn[...], 1, 0) * (1.0 / t_temp)) * b[...]
        d = (p - t * coef[rows, 0:1]).astype(bf16)
        part = dot(d, sn[...], 1, 1)
        prod = dot(ub[rows, :], d, 0, 0)

        if x == 0:
            p_out[...] = prod
        else:
            p_out[...] += prod

        @pl.when(j == 0)
        def _():
            g[rows, :] = part

        @pl.when(j > 0)
        def _():
            g[rows, :] += part

    @pl.when(j == NB - 1)
    def _():
        v = g[...]
        g0_out[...] = jnp.concatenate([v[:, 64 * y : 64 * y + 32] for y in range(NY)], 1)
        g1_out[...] = jnp.concatenate([v[:, 64 * y + 32 : 64 * y + 64] for y in range(NY)], 1)


def grad_pass(ub, tuc, ci, rt, st, b, sn, tn):
    whole = lambda shape: pl.BlockSpec(shape, lambda j: (0,) * len(shape))
    cols = lambda rows: pl.BlockSpec((rows, BLK), lambda j: (0, j))
    return pl.pallas_call(
        grad_kernel,
        grid=(NB,),
        in_specs=[
            whole((SROWS, K)),
            whole((SROWS, K)),
            whole((SROWS, 1)),
            whole((NX, TB_DEV)),
            whole((16, 128)),
            cols(1),
            cols(K),
            cols(K),
        ],
        out_specs=[cols(K), whole((SROWS, 128)), whole((SROWS, 128))],
        out_shape=[
            jax.ShapeDtypeStruct((K, COLS), f32),
            jax.ShapeDtypeStruct((SROWS, 128), f32),
            jax.ShapeDtypeStruct((SROWS, 128), f32),
        ],
        scratch_shapes=[pltpu.VMEM((SROWS, K), f32), pltpu.VMEM((SROWS, 128), f32)],
        compiler_params=pltpu.CompilerParams(vmem_limit_bytes=VMEM_LIMIT),
        name="dlog_products",
    )(ub, tuc, ci, rt, st, b, sn, tn)


def shift(v, axis, size, d):
    return lax.ppermute(v, axis, [(i, (i + d) % size) for i in range(size)])


def exchange(v, axes):
    return lax.all_to_all(v, axes, 0, 0, tiled=False)


def gather_x(v, ix):
    out = jnp.zeros((NX,) + v.shape, v.dtype)
    out = lax.dynamic_update_slice(out, v[None], (ix,) + (0,) * v.ndim)
    for d in (1, NX - 1, 2):
        got = shift(v, "x", NX, d)
        out = lax.dynamic_update_slice(out, got[None], ((ix - d) % NX,) + (0,) * v.ndim)
    return out


def proto_scatter(p, iz):
    w = p.reshape(NX, NZ, 8, COLS)

    def part(d):
        return lax.dynamic_slice(w, (0, (iz + d) % NZ, 0, 0), (NX, 1, 8, COLS))[:, 0]

    up = part(4)
    for d in (3, 2, 1):
        up = shift(up, "z", NZ, 1) + part(d)
    down = part(-3)
    for d in (2, 1):
        down = shift(down, "z", NZ, -1) + part(-d)
    total = part(0) + shift(up, "z", NZ, 1) + shift(down, "z", NZ, -1)
    got = exchange(total, ("x",))
    return jnp.concatenate([got[x] for x in range(NX)], axis=1)


def feat_sum(g0, g1, ix, iy, ic):
    keep = jnp.where(ic == 0, g0, g1)
    give = jnp.where(ic == 0, g1, g0)
    half = keep + shift(give, "c", NC, 1)
    w = half.reshape(NX, SB_DEV, 128)

    def part(d):
        return lax.dynamic_slice(w, ((ix + d) % NX, 0, 0), (1, SB_DEV, 128))[0]

    far, mid = part(2), SB_DEV // 2
    got_up = shift(far[:mid], "x", NX, 1)
    got_down = shift(far[mid:], "x", NX, -1)
    up = part(1)
    up = jnp.concatenate([up[:mid] + got_up, up[mid:]], 0)
    down = part(-1)
    down = jnp.concatenate([down[:mid], down[mid:] + got_down], 0)
    total = part(0) + shift(up, "x", NX, 1) + shift(down, "x", NX, -1)
    w = total.reshape(SB_DEV, NY, 32).transpose(1, 0, 2)

    def share(d):
        return lax.dynamic_slice(w, ((iy + d) % NY, 0, 0), (1, SB_DEV, 32))[0]

    out = share(0)
    for d in (1, NY - 1, 2):
        out = out + shift(share(d), "y", NY, d)
    return out


def shards(teacher_feat, student_feat, teacher_weight, student_weight, crop_to_image):
    ix, iz = lax.axis_index("x"), lax.axis_index("z")
    iy, ic = lax.axis_index("y"), lax.axis_index("c")
    ixs = jnp.reshape(ix, (1,)).astype(jnp.int32)
    rows = ("x", "y", "c")

    crops = jnp.pad(crop_to_image.astype(f32), (0, 8 * K - SB_DEV)).reshape(8, K)
    packed = jnp.concatenate([teacher_feat.astype(f32), crops], 0)
    tf_all = exchange(jnp.broadcast_to(packed[None], (NX,) + packed.shape), ("x",))
    sf32 = student_feat.astype(f32)
    sf_all = gather_x(sf32, ix)
    ci = tf_all[:, TB_DEV : TB_DEV + 2, :].reshape(NX, 2 * K)[:, :SB_DEV]
    ci = ci.reshape(SROWS, 1).astype(jnp.int32)

    e, c_parts, tn, tu = teacher_pass(ixs, tf_all, teacher_weight)
    ub, tuc, sn, sums = student_pass(ixs, sf_all, ci, tu, student_weight)

    for step in range(ITERS):
        b, r_parts = row_pass(exchange(c_parts, ("z",)), e)
        if step < ITERS - 1:
            r_parts = exchange(r_parts, rows)
            c_parts = col_pass(r_parts, e)
        else:
            wide = jnp.broadcast_to(sums[None], (NROW, 16, 128))
            both = exchange(jnp.concatenate([r_parts, wide], 1), rows).sum(0)
    rt = both[:3].reshape(NX, TB_DEV)
    proto, g0, g1 = grad_pass(ub, tuc, ci, rt, both[8:], b.reshape(1, COLS), sn, tn)

    proto_grad = proto_scatter(proto, iz)
    g = feat_sum(g0, g1, ix, iy, ic)
    inverse = unit_scale(sf32)
    mine = (iy * NC + ic) * 32
    u = lax.dynamic_slice(sf32, (0, mine), (SB_DEV, 32)) * inverse
    along = jnp.pad(jnp.sum(u * g, axis=1), (0, 1024 - SB_DEV)).reshape(8, 128)
    along = exchange(jnp.broadcast_to(along[None], (NY * NC, 8, 128)), ("y", "c")).sum(0)
    along = along.reshape(1024)[:SB_DEV]
    feat_grad = (g - u * along[:, None]) * inverse
    return (feat_grad, proto_grad)


def solution(mesh):
    split = Mesh(mesh.devices.reshape(NX, NZ, NY, NC), ("x", "z", "y", "c"))
    dp, mp = ("x", "z"), ("y", "c")
    return jax.shard_map(
        shards,
        mesh=split,
        in_specs=(P(dp, None), P(dp, None), P(None, mp), P(None, mp), P(dp)),
        out_specs=(P(dp, mp), P(dp, mp)),
        check_vma=False,
    )
```

```python
import functools

import jax
import jax.numpy as jnp
from jax import lax
from jax.experimental import pallas as pl
from jax.experimental.pallas import tpu as pltpu
from jax.sharding import Mesh
from jax.sharding import PartitionSpec as P

K = 256
P_SIZE = 65536
TB_DEV = 96
TB_TOTAL = 3072
ITERS = 3
SB_DEV = 480
NX, NZ, NY, NC = 4, 8, 4, 2
NROW = NX * NY * NC
COLS = P_SIZE // NROW
LG = COLS // 128
TROWS = NX * TB_DEV
SROWS = NX * SB_DEV

eps = 1e-06
t_temp = 0.07
s_temp = 0.1
loss_scale = 1024.0

f32 = jnp.float32
bf16 = jnp.bfloat16
MIB = 1024 * 1024
GRAD_MIB = 28
LOG2E = 1.4426950408889634
HALF = COLS // 2


def unit_scale(v):
    return lax.rsqrt(jnp.sum(v * v, axis=1, keepdims=True) + eps)


def norm_columns(w):
    v = w.astype(f32)
    return (v * lax.rsqrt(jnp.sum(v * v, axis=0, keepdims=True) + eps)).astype(bf16)


def dot(a, b, ca, cb):
    return lax.dot_general(a, b, (((ca,), (cb,)), ((), ())), preferred_element_type=f32)


def lane_groups(v):
    return jnp.concatenate([v[:, 128 * k : 128 * (k + 1)] for k in range(v.shape[1] // 128)], 0)


def in_hbm(v):
    return pltpu.with_memory_space_constraint(v, pltpu.HBM)


def in_vmem(v):
    return pltpu.with_memory_space_constraint(v, pltpu.VMEM)


def cost(us):
    return pl.CostEstimate(flops=int(us * 1e9), bytes_accessed=0, transcendentals=0)


def call(kernel, out_shape, name, mib, scratch=(), us=1):
    return pl.pallas_call(
        kernel,
        out_shape=out_shape,
        cost_estimate=cost(us),
        scratch_shapes=list(scratch),
        compiler_params=pltpu.CompilerParams(vmem_limit_bytes=mib * MIB),
        name=name,
    )


def arr(*shape, dtype=f32):
    return jax.ShapeDtypeStruct(shape, dtype)


def norm_kernel(at, w, *outs):
    n = norm_columns(w[...])
    for out in outs:
        out[...] = n


def norm_pass(at, w, outs, name):
    return pl.pallas_call(
        norm_kernel,
        grid_spec=pltpu.PrefetchScalarGridSpec(
            num_scalar_prefetch=1,
            grid=(2,),
            in_specs=[pl.BlockSpec((K, 1024), lambda j, at: (0, at[0] * 2 + j))],
            out_specs=[pl.BlockSpec((K, 1024), lambda j, at: (0, j))] * len(outs),
        ),
        out_shape=outs,
        cost_estimate=cost(2),
        compiler_params=pltpu.CompilerParams(vmem_limit_bytes=12 * MIB),
        name=name,
    )(at, in_hbm(w))


def pack_kernel(at, sf, crops, own, half):
    n = SB_DEV // NC
    own[:SB_DEV, :] = sf[...].astype(f32)
    own[SB_DEV:, :] = crops[...]
    half[:n, :] = own[pl.ds(pl.multiple_of(at[1] * n, 8), n), :]
    row = jnp.where(at[1] == 0, crops[0:1, :], crops[1:2, :])
    half[n:, :] = jnp.broadcast_to(row, (8, K))


def pack_pass(at, sf, crops):
    outs = [pltpu.HBM((SB_DEV + 8, K), f32), pltpu.HBM((SB_DEV // NC + 8, K), f32)]
    return small_call(pack_kernel, outs, "pack_rows", at, sf, crops)


def exponentials(tu, tn, j):
    return jnp.exp2(dot(tu[...], tn[:, 512 * j : 512 * (j + 1)], 1, 0) * (LOG2E / t_temp))


def put_columns(c_out, j, c):
    for k in range(4):
        part = c[None, :, 128 * k : 128 * (k + 1)]
        c_out[:, 4 * j + k : 4 * j + k + 1, :] = jnp.broadcast_to(part, (NZ, 1, 128))


def teacher_kernel(tf, tn, c_out, tu_out):
    for x in range(NX):
        v = tf[x]
        tu_out[x * TB_DEV : (x + 1) * TB_DEV, :] = (v * unit_scale(v)).astype(bf16)
    for j in range(COLS // 512):
        put_columns(c_out, j, jnp.sum(exponentials(tu_out, tn, j), axis=0, keepdims=True))


def teacher_pass(tf_all, tn):
    outs = [arr(NZ, LG, 128), pltpu.VMEM((TROWS, K), bf16)]
    return call(teacher_kernel, outs, "teacher_scores", 12)(tf_all, in_vmem(tn))


def row_kernel(tail, c_parts, tu, tn, *refs):
    if tail:
        extra, b_out, r_out = refs
        r_out[:, 8:, :] = jnp.broadcast_to(extra[...][None], (NROW, 16, 128))
    else:
        (r_out,) = refs
    b = 1.0 / (jnp.sum(c_parts[...], axis=0) * P_SIZE)
    if tail:
        b_out[...] = b
    acc = None
    for j in range(COLS // 512):
        e = exponentials(tu, tn, j)
        for k in range(4):
            part = e[:, 128 * k : 128 * (k + 1)] * b[4 * j + k : 4 * j + k + 1, :]
            acc = part if acc is None else acc + part
    r = [jnp.sum(acc[128 * k : 128 * (k + 1), :].T, axis=0, keepdims=True) for k in range(3)]
    r = jnp.concatenate(r + [jnp.ones((5, 128), f32)], 0)
    r_out[:, :8, :] = jnp.broadcast_to(r[None], (NROW, 8, 128))


def row_pass(c_parts, tu, tn, *extra):
    tail = len(extra) > 0
    outs = [arr(LG, 128), arr(NROW, 24, 128)] if tail else [arr(NROW, 8, 128)]
    name = "last_row_sums" if tail else "row_sums"
    kernel = functools.partial(row_kernel, tail)
    return call(kernel, outs, name, 12)(c_parts, in_vmem(tu), in_vmem(tn), *extra)


def col_kernel(r_parts, tu, tn, c_out):
    a = 1.0 / (jnp.sum(r_parts[...], axis=0) * TB_TOTAL)
    wide = jnp.concatenate([jnp.broadcast_to(a[k : k + 1, :], (128, 128)).T for k in range(3)], 0)
    wide = jnp.concatenate([wide] * 4, 1)
    for j in range(COLS // 512):
        put_columns(c_out, j, jnp.sum(exponentials(tu, tn, j) * wide, axis=0, keepdims=True))


def col_pass(r_parts, tu, tn):
    return call(col_kernel, arr(NZ, LG, 128), "col_sums", 12)(r_parts, in_vmem(tu), in_vmem(tn))


def rows_kernel(at, own, mine_1, mine_2, mine_3, core_1, core_2, core_3, tu, *refs):
    ub_out, ubt_out, ut_out, tuc_out, crop_out, mine_out, sf = refs
    ix, ic = at[0], at[1]
    half = SB_DEV // NC
    spare = jnp.zeros((1, 512 - SB_DEV), f32)
    crop_out[...] = jnp.zeros_like(crop_out)
    sf[ix] = own[:SB_DEV, :]
    row = jnp.concatenate([own[SB_DEV : SB_DEV + 1, :half], own[SB_DEV + 1 : SB_DEV + 2, :half], spare], 1)
    crop_out[ix, 0:1, :] = row
    for d, mine, core in ((1, mine_1, core_1), (2, mine_2, core_2), (3, mine_3, core_3)):
        x = lax.rem(ix + NX - d, NX)
        sf[x, pl.ds(pl.multiple_of(ic * half, 8), half), :] = mine[:half, :]
        sf[x, pl.ds(pl.multiple_of((1 - ic) * half, 8), half), :] = core[:half, :]
        m, c = mine[half : half + 1, :half], core[half : half + 1, :half]
        row = jnp.concatenate([jnp.where(ic == 0, m, c), jnp.where(ic == 0, c, m), spare], 1)
        crop_out[x, 0:1, :] = row
    for x in range(NX):
        rows = slice(x * SB_DEV, (x + 1) * SB_DEV)
        v = sf[x]
        scale = unit_scale(v)
        u = v * scale
        ub_out[rows, :] = u.astype(bf16)
        crop_out[x, 1:2, :SB_DEV] = jnp.broadcast_to(scale, (SB_DEV, 128)).T[0:1, :]
        ut = u.T
        ut_out[x] = ut
        ubt_out[x] = ut.astype(bf16)
        row = lax.broadcasted_iota(jnp.int32, (TB_DEV, SB_DEV), 0)
        pick = row == crop_out[x, 0:1, :SB_DEV].astype(jnp.int32)
        pick = jnp.where(pick, 1.0, 0.0).astype(bf16)
        tuc_out[rows, :] = dot(pick, tu[x * TB_DEV : (x + 1) * TB_DEV, :], 0, 0).astype(bf16)
    mine_out[:32, :] = ut_out[ix, pl.ds(pl.multiple_of((at[3] * NC + ic) * 32, 8), 32), :]
    mine_out[32:, :] = jnp.broadcast_to(crop_out[ix, 1:2, :SB_DEV], (8, SB_DEV))


def rows_pass(at, own, mine, core, tu):
    whole = lambda shape: pl.BlockSpec(shape, lambda i, at: (0,) * len(shape))
    half = whole((SB_DEV // NC + 8, K))
    outs = [
        arr(SROWS, K, dtype=bf16),
        arr(NX, K, SB_DEV, dtype=bf16),
        arr(NX, K, SB_DEV),
        arr(SROWS, K, dtype=bf16),
        arr(NX, 8, 512),
        arr(40, SB_DEV),
    ]
    return pl.pallas_call(
        rows_kernel,
        grid_spec=pltpu.PrefetchScalarGridSpec(
            num_scalar_prefetch=1,
            grid=(1,),
            in_specs=[whole((SB_DEV + 8, K))] + [half] * 6 + [whole((TROWS, K))],
            out_specs=[whole(v.shape) for v in outs],
            scratch_shapes=[pltpu.VMEM((NX, SB_DEV, K), f32)],
        ),
        out_shape=[pltpu.HBM(v.shape, v.dtype) for v in outs],
        cost_estimate=cost(3),
        compiler_params=pltpu.CompilerParams(vmem_limit_bytes=20 * MIB),
        name="student_units",
    )(at, *[in_hbm(v) for v in (own, *mine, *core)], tu)


def student_kernel(ub, sn, rs_out):
    for x in range(NX):
        rows = slice(x * SB_DEV, (x + 1) * SB_DEV)
        total = None
        for j in range(COLS // 512):
            e = jnp.exp2(dot(ub[rows, :], sn[:, 512 * j : 512 * (j + 1)], 1, 0) * (LOG2E / s_temp))
            for k in range(4):
                part = e[:, 128 * k : 128 * (k + 1)]
                total = part if total is None else total + part
        for k in range(4):
            part = total[128 * k : min(128 * (k + 1), SB_DEV), :].T
            part = jnp.sum(part, axis=0, keepdims=True)
            if part.shape[1] < 128:
                part = jnp.concatenate([part, jnp.ones((1, 128 - part.shape[1]), f32)], 1)
            rs_out[4 * x + k : 4 * x + k + 1, :] = part


def student_pass(ub, sn):
    return call(student_kernel, arr(16, 128), "student_sums", 14, us=3)(ub, sn)


def factors(crops, parts, coef):
    total = jnp.sum(parts[...], axis=0)
    a = (loss_scale / s_temp) / total[:3]
    a = jnp.concatenate([a[0:1], a[1:2], a[2:3]], 1)
    s = (loss_scale / s_temp) / total[8:]
    row = lax.broadcasted_iota(jnp.int32, (TB_DEV, SB_DEV), 0)
    lane = lax.broadcasted_iota(jnp.int32, (128, 128), 1)
    for x in range(NX):
        ax = jnp.concatenate([a[:, x * TB_DEV : (x + 1) * TB_DEV], jnp.zeros((1, 32), f32)], 1)
        ax = jnp.broadcast_to(ax, (128, 128)).T[:TB_DEV, 0:1]
        pick = row == crops[x, 0:1, :SB_DEV].astype(jnp.int32)
        ac = jnp.sum(jnp.where(pick, ax, 0.0), axis=0, keepdims=True)
        ac = jnp.concatenate([ac, jnp.zeros((1, 512 - SB_DEV), f32)], 1)
        for k in range(4):
            ak = jnp.broadcast_to(ac[:, 128 * k : 128 * (k + 1)], (128, 128)).T
            sk = jnp.broadcast_to(s[4 * x + k : 4 * x + k + 1, :], (128, 128)).T
            n = min(128, SB_DEV - 128 * k)
            both = jnp.where(lane == 0, ak, sk)
            coef[x * SB_DEV + 128 * k : x * SB_DEV + 128 * k + n, :] = both[:n]


def grad_half(h, iz, ub, ubt, tuc, coef, b, sn, tn, g_in, g_out, p, p_outs):
    cols = slice(h * HALF, (h + 1) * HALF)
    bh = jnp.concatenate([b[k : k + 1, :] for k in range(h * LG // 2, (h + 1) * LG // 2)], 1)
    for x in range(NX):
        rows = slice(x * SB_DEV, (x + 1) * SB_DEV)
        q = jnp.exp2(dot(ub[rows, :], sn[:, cols], 1, 0) * (LOG2E / s_temp)) * coef[rows, 1:2]
        t = jnp.exp2(dot(tuc[rows, :], tn[:, cols], 1, 0) * (LOG2E / t_temp)) * bh
        d = (q - t * coef[rows, 0:1]).astype(bf16)
        prod = dot(ubt[x], d, 1, 0)
        if x == 0:
            p[...] = prod
        else:
            p[...] += prod
        part = dot(d, sn[:, cols], 1, 1)
        g_out[rows, :] = part if g_in is None else g_in[rows, :] + part
    for d in range(NZ):
        z = lax.rem(iz + d, NZ)
        for x in range(NX):
            p_outs[d][x] = p[pl.ds(pl.multiple_of(x * 64 + z * 8, 8), 8), :]


def first_kernel(at, crops, parts, ub, ubt, tuc, b, sn, tn, *refs):
    *p_outs, g_out, coef, p = refs
    factors(crops, parts, coef)
    grad_half(0, at[2], ub, ubt, tuc, coef, b, sn, tn, None, g_out, p, p_outs)


def second_kernel(at, coef, g_in, ut, ub, ubt, tuc, b, sn, tn, *refs):
    *p_outs, g_out, p, g = refs
    grad_half(1, at[2], ub, ubt, tuc, coef, b, sn, tn, g_in, g, p, p_outs)
    for x in range(NX):
        gt = g[x * SB_DEV : (x + 1) * SB_DEV, :].T
        along = jnp.sum(ut[x] * gt, axis=0, keepdims=True)
        along = jnp.broadcast_to(along, (8, SB_DEV))
        for m in range(NY * NC):
            g_out[x * NY * NC + m, :32, :] = gt[32 * m : 32 * (m + 1), :]
            g_out[x * NY * NC + m, 32:, :] = along


def grad_call(kernel, outs, name, scratch, at, *args):
    whole = lambda v: pl.BlockSpec(v.shape, lambda i, at, n=len(v.shape): (0,) * n)
    return pl.pallas_call(
        kernel,
        grid_spec=pltpu.PrefetchScalarGridSpec(
            num_scalar_prefetch=1,
            grid=(1,),
            in_specs=[whole(v) for v in args],
            out_specs=[whole(arr(NX, 8, HALF))] * NZ + [whole(v) for v in outs],
            scratch_shapes=[pltpu.VMEM((K, HALF), f32)] + scratch,
        ),
        out_shape=[pltpu.HBM((NX, 8, HALF), f32)] * NZ + outs,
        cost_estimate=cost(8),
        compiler_params=pltpu.CompilerParams(vmem_limit_bytes=GRAD_MIB * MIB),
        name=name,
    )(at, *args)


def first_pass(at, crops, parts, *common):
    outs = [arr(SROWS, K), arr(SROWS, 128)]
    *p, g, coef = grad_call(first_kernel, outs, "first_half", [], at, crops, parts, *common)
    return p, g, coef


def second_pass(at, coef, g, ut, *common):
    outs = [pltpu.HBM((NROW, 40, SB_DEV), f32)]
    scratch = [pltpu.VMEM((SROWS, K), f32)]
    *p, g = grad_call(second_kernel, outs, "second_half", scratch, at, coef, g, ut, *common)
    return p, g


def feat_kernel(parts, mine, out):
    g = jnp.sum(parts[...], axis=0)
    out[...] = (g[:32] - mine[:32, :] * g[32:33]) * mine[32:33, :]


def feat_pass(parts, mine):
    return call(feat_kernel, arr(32, SB_DEV), "feat_grad", 8)(parts, mine)


def merge_kernel(at, p0, u0, d0, p1, u1, d1, *outs):
    for d in range(NX):
        x = lax.rem(at[0] + d, NX)
        outs[d][:, :HALF] = p0[x] + u0[x] + d0[x]
        outs[d][:, HALF:] = p1[x] + u1[x] + d1[x]


def merge_pass(at, *args):
    return small_call(merge_kernel, [arr(8, COLS)] * NX, "merge_sums", at, *args)


def proto_kernel(at, *refs):
    out = refs[NX]
    for d in range(NX):
        x = lax.rem(at[0] + NX - d, NX)
        out[:, pl.ds(pl.multiple_of(x * COLS, 128), COLS)] = refs[d][...]


def proto_pass(at, *args):
    return small_call(proto_kernel, [arr(8, NX * COLS)], "proto_grad", at, *args)[0]


def small_call(kernel, outs, name, at, *args):
    whole = lambda v: pl.BlockSpec(v.shape, lambda i, at, n=len(v.shape): (0,) * n)
    return pl.pallas_call(
        kernel,
        grid_spec=pltpu.PrefetchScalarGridSpec(
            num_scalar_prefetch=1,
            grid=(1,),
            in_specs=[whole(v) for v in args],
            out_specs=[whole(v) for v in outs],
        ),
        out_shape=outs,
        cost_estimate=cost(1),
        compiler_params=pltpu.CompilerParams(vmem_limit_bytes=6 * MIB),
        name=name,
    )(at, *args)


def shift(v, axis, size, d):
    return lax.ppermute(v, axis, [(i, (i + d) % size) for i in range(size)])


def exchange(v, axes):
    return lax.all_to_all(v, axes, 0, 0, tiled=False)


def shards(teacher_feat, student_feat, teacher_weight, student_weight, crop_to_image):
    ix, iz = lax.axis_index("x"), lax.axis_index("z")
    iy, ic = lax.axis_index("y"), lax.axis_index("c")
    at = jnp.stack([ix, ic, iz, iy]).astype(jnp.int32)
    group = ("x", "y", "c")
    together = lax.optimization_barrier

    tf_all = jnp.broadcast_to(teacher_feat.astype(f32)[None], (NX, TB_DEV, K))
    tf_all = exchange(tf_all, ("x",))
    rows = SB_DEV // NC
    crops = jnp.pad(crop_to_image.astype(f32).reshape(NC, rows), ((0, 6), (0, K - rows)))
    own, half = pack_pass(at, student_feat, crops)
    mine = [shift(half, "x", NX, d) for d in (1, 3, 2)]
    share = (K, COLS)
    tn, tv = norm_pass(
        at, teacher_weight, [pltpu.HBM(share, bf16), pltpu.VMEM(share, bf16)], "teacher_norm"
    )
    tf_all, tn, tv, own = together((tf_all, tn, tv, own))

    c_parts, tu = teacher_pass(tf_all, tv)
    r_parts = row_pass(exchange(c_parts, ("z",)), tu, tv)[0]
    r_parts, at_1 = together((r_parts, at))
    r_parts = exchange(r_parts, group)
    (sn,) = norm_pass(at_1, student_weight, [pltpu.HBM(share, bf16)], "student_norm")
    c_parts, sn, *mine = together((col_pass(r_parts, tu, tv), sn, *mine))
    c_parts = exchange(c_parts, ("z",))
    core = [shift(v, "c", NC, 1) for v in mine]
    c_parts, *core = together((c_parts, *core))
    r_parts, tu = together((row_pass(c_parts, tu, tv)[0], tu))
    r_parts = exchange(r_parts, group)
    mine, core = (mine[0], mine[2], mine[1]), (core[0], core[2], core[1])
    ub, ubt, ut, tuc, crops, mine = rows_pass(at, own, mine, core, tu)
    r_parts, ub, ubt, ut, tuc = together((r_parts, ub, ubt, ut, tuc))
    c_parts, ub = together((col_pass(r_parts, tu, tv), ub))
    c_parts = exchange(c_parts, ("z",))
    sums = student_pass(ub, sn)
    b, parts = row_pass(c_parts, tu, tv, sums)
    parts = exchange(parts, group)

    common = (ub, ubt, tuc, b, sn, tn)
    p0, g, coef = first_pass(at, crops, parts, *common)
    up = lambda v: shift(v, "z", NZ, 1)
    down = lambda v: shift(v, "z", NZ, -1)
    u0, d0 = up(p0[4]), down(p0[5])
    p1, g = second_pass(at, coef, g, ut, *common)
    u0, d0, g, *p1 = together((u0, d0, g, *p1))
    g = exchange(g, group)
    u1, d1 = up(p1[3]), down(p1[4])
    for k in (3, 2):
        u0, d0 = up(u0 + p0[k]), down(d0 + p0[9 - k])
        u1, d1 = up(u1 + p1[k - 1]), down(d1 + p1[8 - k])
    u0, d1 = up(u0 + p0[1]), down(d1 + p1[7])
    own, *give = merge_pass(at, p0[0], u0, d0, p1[0], u1, d1)
    got = [shift(v, "x", NX, d) for v, d in zip(give, (1, 2, 3))]
    proto_grad = proto_pass(at, own, *got)
    feat_grad = feat_pass(g, mine).T
    return (feat_grad, proto_grad)


def solution(mesh):
    split = Mesh(mesh.devices.reshape(NX, NZ, NY, NC), ("x", "z", "y", "c"))
    dp, mp = ("x", "z"), ("y", "c")
    return jax.shard_map(
        shards,
        mesh=split,
        in_specs=(P(dp, None), P(dp, None), P(None, mp), P(None, mp), P(dp)),
        out_specs=(P(dp, mp), P(dp, mp)),
        check_vma=False,
    )
```

```python
import functools

import jax
import jax.numpy as jnp
from jax import lax
from jax.experimental import pallas as pl
from jax.experimental.pallas import tpu as pltpu
from jax.sharding import Mesh
from jax.sharding import PartitionSpec as P

K = 256
P_SIZE = 65536
TB_DEV = 96
TB_TOTAL = 3072
ITERS = 3
SB_DEV = 480
NX, NZ, NY, NC = 4, 8, 4, 2
NROW = NX * NY * NC
COLS = P_SIZE // NROW
LG = COLS // 128
TROWS = NX * TB_DEV
SROWS = NX * SB_DEV

eps = 1e-06
t_temp = 0.07
s_temp = 0.1
loss_scale = 1024.0

f32 = jnp.float32
bf16 = jnp.bfloat16
MIB = 1024 * 1024
GRAD_MIB = 28
LOG2E = 1.4426950408889634
HALF = COLS // 2


def unit_scale(v):
    return lax.rsqrt(jnp.sum(v * v, axis=1, keepdims=True) + eps)


def norm_columns(w):
    v = w.astype(f32)
    return (v * lax.rsqrt(jnp.sum(v * v, axis=0, keepdims=True) + eps)).astype(bf16)


def dot(a, b, ca, cb):
    return lax.dot_general(a, b, (((ca,), (cb,)), ((), ())), preferred_element_type=f32)


def lane_groups(v):
    return jnp.concatenate([v[:, 128 * k : 128 * (k + 1)] for k in range(v.shape[1] // 128)], 0)


def in_hbm(v):
    return pltpu.with_memory_space_constraint(v, pltpu.HBM)


def in_vmem(v):
    return pltpu.with_memory_space_constraint(v, pltpu.VMEM)


def cost(us):
    return pl.CostEstimate(flops=int(us * 1e9), bytes_accessed=0, transcendentals=0)


def call(kernel, out_shape, name, mib, scratch=(), us=1):
    return pl.pallas_call(
        kernel,
        out_shape=out_shape,
        cost_estimate=cost(us),
        scratch_shapes=list(scratch),
        compiler_params=pltpu.CompilerParams(vmem_limit_bytes=mib * MIB),
        name=name,
    )


def arr(*shape, dtype=f32):
    return jax.ShapeDtypeStruct(shape, dtype)


def norm_kernel(at, w, *outs):
    n = norm_columns(w[...])
    for out in outs:
        out[...] = n


def norm_pass(at, w, outs, name):
    return pl.pallas_call(
        norm_kernel,
        grid_spec=pltpu.PrefetchScalarGridSpec(
            num_scalar_prefetch=1,
            grid=(2,),
            in_specs=[pl.BlockSpec((K, 1024), lambda j, at: (0, at[0] * 2 + j))],
            out_specs=[pl.BlockSpec((K, 1024), lambda j, at: (0, j))] * len(outs),
        ),
        out_shape=outs,
        cost_estimate=cost(2),
        compiler_params=pltpu.CompilerParams(vmem_limit_bytes=12 * MIB),
        name=name,
    )(at, in_hbm(w))


def pack_kernel(at, sf, crops, own, half):
    n = SB_DEV // NC
    own[:SB_DEV, :] = sf[...].astype(f32)
    own[SB_DEV:, :] = crops[...]
    half[:n, :] = own[pl.ds(pl.multiple_of(at[1] * n, 8), n), :]
    row = jnp.where(at[1] == 0, crops[0:1, :], crops[1:2, :])
    half[n:, :] = jnp.broadcast_to(row, (8, K))


def pack_pass(at, sf, crops):
    outs = [pltpu.HBM((SB_DEV + 8, K), f32), pltpu.HBM((SB_DEV // NC + 8, K), f32)]
    return small_call(pack_kernel, outs, "pack_rows", at, sf, crops)


def exponentials(tu, tn, j):
    return jnp.exp2(dot(tu[...], tn[:, 512 * j : 512 * (j + 1)], 1, 0) * (LOG2E / t_temp))


def put_columns(c_out, j, c):
    for k in range(4):
        part = c[None, :, 128 * k : 128 * (k + 1)]
        c_out[:, 4 * j + k : 4 * j + k + 1, :] = jnp.broadcast_to(part, (NZ, 1, 128))


def teacher_kernel(tf, tn, c_out, tu_out):
    for x in range(NX):
        v = tf[x]
        tu_out[x * TB_DEV : (x + 1) * TB_DEV, :] = (v * unit_scale(v)).astype(bf16)
    for j in range(COLS // 512):
        put_columns(c_out, j, jnp.sum(exponentials(tu_out, tn, j), axis=0, keepdims=True))


def teacher_pass(tf_all, tn):
    outs = [arr(NZ, LG, 128), pltpu.VMEM((TROWS, K), bf16)]
    return call(teacher_kernel, outs, "teacher_scores", 12)(tf_all, in_vmem(tn))


def row_kernel(tail, c_parts, tu, tn, *refs):
    if tail:
        extra, b_out, r_out = refs
        r_out[:, 8:, :] = jnp.broadcast_to(extra[...][None], (NROW, 16, 128))
    else:
        (r_out,) = refs
    b = 1.0 / (jnp.sum(c_parts[...], axis=0) * P_SIZE)
    if tail:
        b_out[...] = b
    acc = None
    for j in range(COLS // 512):
        e = exponentials(tu, tn, j)
        for k in range(4):
            part = e[:, 128 * k : 128 * (k + 1)] * b[4 * j + k : 4 * j + k + 1, :]
            acc = part if acc is None else acc + part
    r = [jnp.sum(acc[128 * k : 128 * (k + 1), :].T, axis=0, keepdims=True) for k in range(3)]
    r = jnp.concatenate(r + [jnp.ones((5, 128), f32)], 0)
    r_out[:, :8, :] = jnp.broadcast_to(r[None], (NROW, 8, 128))


def row_pass(c_parts, tu, tn, *extra):
    tail = len(extra) > 0
    outs = [arr(LG, 128), arr(NROW, 24, 128)] if tail else [arr(NROW, 8, 128)]
    name = "last_row_sums" if tail else "row_sums"
    kernel = functools.partial(row_kernel, tail)
    return call(kernel, outs, name, 12)(c_parts, in_vmem(tu), in_vmem(tn), *extra)


def col_kernel(r_parts, tu, tn, c_out):
    a = 1.0 / (jnp.sum(r_parts[...], axis=0) * TB_TOTAL)
    wide = jnp.concatenate([jnp.broadcast_to(a[k : k + 1, :], (128, 128)).T for k in range(3)], 0)
    wide = jnp.concatenate([wide] * 4, 1)
    for j in range(COLS // 512):
        put_columns(c_out, j, jnp.sum(exponentials(tu, tn, j) * wide, axis=0, keepdims=True))


def col_pass(r_parts, tu, tn):
    return call(col_kernel, arr(NZ, LG, 128), "col_sums", 12)(r_parts, in_vmem(tu), in_vmem(tn))


def rows_kernel(at, own, mine_1, mine_2, mine_3, core_1, core_2, core_3, tu, *refs):
    ub_out, ubt_out, ut_out, tuc_out, crop_out, mine_out, sf = refs
    ix, ic = at[0], at[1]
    half = SB_DEV // NC
    spare = jnp.zeros((1, 512 - SB_DEV), f32)
    crop_out[...] = jnp.zeros_like(crop_out)
    sf[ix] = own[:SB_DEV, :]
    row = jnp.concatenate([own[SB_DEV : SB_DEV + 1, :half], own[SB_DEV + 1 : SB_DEV + 2, :half], spare], 1)
    crop_out[ix, 0:1, :] = row
    for d, mine, core in ((1, mine_1, core_1), (2, mine_2, core_2), (3, mine_3, core_3)):
        x = lax.rem(ix + NX - d, NX)
        sf[x, pl.ds(pl.multiple_of(ic * half, 8), half), :] = mine[:half, :]
        sf[x, pl.ds(pl.multiple_of((1 - ic) * half, 8), half), :] = core[:half, :]
        m, c = mine[half : half + 1, :half], core[half : half + 1, :half]
        row = jnp.concatenate([jnp.where(ic == 0, m, c), jnp.where(ic == 0, c, m), spare], 1)
        crop_out[x, 0:1, :] = row
    for x in range(NX):
        rows = slice(x * SB_DEV, (x + 1) * SB_DEV)
        v = sf[x]
        scale = unit_scale(v)
        u = v * scale
        ub_out[rows, :] = u.astype(bf16)
        crop_out[x, 1:2, :SB_DEV] = jnp.broadcast_to(scale, (SB_DEV, 128)).T[0:1, :]
        ut = u.T
        ut_out[x] = ut
        ubt_out[x] = ut.astype(bf16)
        row = lax.broadcasted_iota(jnp.int32, (TB_DEV, SB_DEV), 0)
        pick = row == crop_out[x, 0:1, :SB_DEV].astype(jnp.int32)
        pick = jnp.where(pick, 1.0, 0.0).astype(bf16)
        tuc_out[rows, :] = dot(pick, tu[x * TB_DEV : (x + 1) * TB_DEV, :], 0, 0).astype(bf16)
    mine_out[:32, :] = ut_out[ix, pl.ds(pl.multiple_of((at[3] * NC + ic) * 32, 8), 32), :]
    mine_out[32:, :] = jnp.broadcast_to(crop_out[ix, 1:2, :SB_DEV], (8, SB_DEV))


def rows_pass(at, own, mine, core, tu):
    whole = lambda shape: pl.BlockSpec(shape, lambda i, at: (0,) * len(shape))
    half = whole((SB_DEV // NC + 8, K))
    outs = [
        arr(SROWS, K, dtype=bf16),
        arr(NX, K, SB_DEV, dtype=bf16),
        arr(NX, K, SB_DEV),
        arr(SROWS, K, dtype=bf16),
        arr(NX, 8, 512),
        arr(40, SB_DEV),
    ]
    return pl.pallas_call(
        rows_kernel,
        grid_spec=pltpu.PrefetchScalarGridSpec(
            num_scalar_prefetch=1,
            grid=(1,),
            in_specs=[whole((SB_DEV + 8, K))] + [half] * 6 + [whole((TROWS, K))],
            out_specs=[whole(v.shape) for v in outs],
            scratch_shapes=[pltpu.VMEM((NX, SB_DEV, K), f32)],
        ),
        out_shape=[pltpu.HBM(v.shape, v.dtype) for v in outs],
        cost_estimate=cost(3),
        compiler_params=pltpu.CompilerParams(vmem_limit_bytes=20 * MIB),
        name="student_units",
    )(at, *[in_hbm(v) for v in (own, *mine, *core)], tu)


def student_kernel(ub, sn, rs_out):
    for x in range(NX):
        rows = slice(x * SB_DEV, (x + 1) * SB_DEV)
        total = None
        for j in range(COLS // 512):
            e = jnp.exp2(dot(ub[rows, :], sn[:, 512 * j : 512 * (j + 1)], 1, 0) * (LOG2E / s_temp))
            for k in range(4):
                part = e[:, 128 * k : 128 * (k + 1)]
                total = part if total is None else total + part
        for k in range(4):
            part = total[128 * k : min(128 * (k + 1), SB_DEV), :].T
            part = jnp.sum(part, axis=0, keepdims=True)
            if part.shape[1] < 128:
                part = jnp.concatenate([part, jnp.ones((1, 128 - part.shape[1]), f32)], 1)
            rs_out[4 * x + k : 4 * x + k + 1, :] = part


def student_pass(ub, sn):
    return call(student_kernel, arr(16, 128), "student_sums", 14, us=3)(ub, sn)


def factors(crops, parts, coef):
    total = jnp.sum(parts[...], axis=0)
    a = (loss_scale / s_temp) / total[:3]
    a = jnp.concatenate([a[0:1], a[1:2], a[2:3]], 1)
    s = (loss_scale / s_temp) / total[8:]
    row = lax.broadcasted_iota(jnp.int32, (TB_DEV, SB_DEV), 0)
    lane = lax.broadcasted_iota(jnp.int32, (128, 128), 1)
    for x in range(NX):
        ax = jnp.concatenate([a[:, x * TB_DEV : (x + 1) * TB_DEV], jnp.zeros((1, 32), f32)], 1)
        ax = jnp.broadcast_to(ax, (128, 128)).T[:TB_DEV, 0:1]
        pick = row == crops[x, 0:1, :SB_DEV].astype(jnp.int32)
        ac = jnp.sum(jnp.where(pick, ax, 0.0), axis=0, keepdims=True)
        ac = jnp.concatenate([ac, jnp.zeros((1, 512 - SB_DEV), f32)], 1)
        for k in range(4):
            ak = jnp.broadcast_to(ac[:, 128 * k : 128 * (k + 1)], (128, 128)).T
            sk = jnp.broadcast_to(s[4 * x + k : 4 * x + k + 1, :], (128, 128)).T
            n = min(128, SB_DEV - 128 * k)
            both = jnp.where(lane == 0, ak, sk)
            coef[x * SB_DEV + 128 * k : x * SB_DEV + 128 * k + n, :] = both[:n]


def grad_half(h, iz, ub, ubt, tuc, coef, b, sn, tn, p, p_outs, take):
    cols = slice(h * HALF, (h + 1) * HALF)
    bh = jnp.concatenate([b[k : k + 1, :] for k in range(h * LG // 2, (h + 1) * LG // 2)], 1)
    for x in range(NX):
        rows = slice(x * SB_DEV, (x + 1) * SB_DEV)
        q = jnp.exp2(dot(ub[rows, :], sn[:, cols], 1, 0) * (LOG2E / s_temp)) * coef[rows, 1:2]
        t = jnp.exp2(dot(tuc[rows, :], tn[:, cols], 1, 0) * (LOG2E / t_temp)) * bh
        d = (q - t * coef[rows, 0:1]).astype(bf16)
        prod = dot(ubt[x], d, 1, 0)
        if x == 0:
            p[...] = prod
        else:
            p[...] += prod
        take(x, rows, dot(d, sn[:, cols], 1, 1))
    for d in range(NZ):
        z = lax.rem(iz + d, NZ)
        for x in range(NX):
            p_outs[d][x] = p[pl.ds(pl.multiple_of(x * 64 + z * 8, 8), 8), :]


def first_kernel(at, crops, parts, ub, ubt, tuc, b, sn, tn, *refs):
    *p_outs, g_out, coef, p = refs
    factors(crops, parts, coef)

    def take(x, rows, part):
        g_out[rows, :] = part

    grad_half(0, at[2], ub, ubt, tuc, coef, b, sn, tn, p, p_outs, take)


def second_kernel(at, coef, g_in, ut, ub, ubt, tuc, b, sn, tn, *refs):
    *p_outs, g_out, p, g, sems = refs
    n, spare = NY * NC, SB_DEV // 32
    out = lambda x: pltpu.make_async_copy(g.at[x], g_out.at[pl.ds(x * n, n)], sems.at[x])

    def take(x, rows, part):
        gt = (g_in[rows, :] + part).T
        along = jnp.sum(ut[x] * gt, axis=0, keepdims=True)
        along = [along[:, 32 * i : 32 * (i + 1)] for i in range(spare)]
        along = jnp.concatenate(along + [jnp.zeros((32 - spare, 32), f32)], 0)
        for m in range(n):
            g[x, m] = jnp.concatenate([gt[32 * m : 32 * (m + 1), :], along], 1)
        out(x).start()

    grad_half(1, at[2], ub, ubt, tuc, coef, b, sn, tn, p, p_outs, take)
    for x in range(NX):
        out(x).wait()


def grad_call(kernel, outs, specs, name, scratch, at, *args):
    whole = lambda v: pl.BlockSpec(v.shape, lambda i, at, n=len(v.shape): (0,) * n)
    return pl.pallas_call(
        kernel,
        grid_spec=pltpu.PrefetchScalarGridSpec(
            num_scalar_prefetch=1,
            grid=(1,),
            in_specs=[whole(v) for v in args],
            out_specs=[whole(arr(NX, 8, HALF))] * NZ + (specs or [whole(v) for v in outs]),
            scratch_shapes=[pltpu.VMEM((K, HALF), f32)] + scratch,
        ),
        out_shape=[pltpu.HBM((NX, 8, HALF), f32)] * NZ + outs,
        cost_estimate=cost(8),
        compiler_params=pltpu.CompilerParams(vmem_limit_bytes=GRAD_MIB * MIB),
        name=name,
    )(at, *args)


def first_pass(at, crops, parts, *common):
    outs = [arr(SROWS, K), arr(SROWS, 128)]
    *p, g, coef = grad_call(first_kernel, outs, None, "first_half", [], at, crops, parts, *common)
    return p, g, coef


def second_pass(at, coef, g, ut, *common):
    outs, specs = [pltpu.HBM((NROW, 32, 512), f32)], [pl.BlockSpec(memory_space=pltpu.HBM)]
    scratch = [pltpu.VMEM((NX, NY * NC, 32, 512), f32), pltpu.SemaphoreType.DMA((NX,))]
    *p, g = grad_call(second_kernel, outs, specs, "second_half", scratch, at, coef, g, ut, *common)
    return p, g


def feat_kernel(parts, mine, out):
    g = jnp.sum(parts[...], axis=0)
    along = jnp.concatenate([g[i : i + 1, SB_DEV:] for i in range(SB_DEV // 32)], 1)
    out[...] = (g[:, :SB_DEV] - mine[:32, :] * along) * mine[32:33, :]


def feat_pass(parts, mine):
    return call(feat_kernel, arr(32, SB_DEV), "feat_grad", 8)(parts, mine)


def merge_kernel(at, p0, u0, d0, p1, u1, d1, *outs):
    for d in range(NX):
        x = lax.rem(at[0] + d, NX)
        outs[d][:, :HALF] = p0[x] + u0[x] + d0[x]
        outs[d][:, HALF:] = p1[x] + u1[x] + d1[x]


def merge_pass(at, *args):
    return small_call(merge_kernel, [arr(8, COLS)] * NX, "merge_sums", at, *args)


def proto_kernel(at, *refs):
    out = refs[NX]
    for d in range(NX):
        x = lax.rem(at[0] + NX - d, NX)
        out[:, pl.ds(pl.multiple_of(x * COLS, 128), COLS)] = refs[d][...]


def proto_pass(at, *args):
    return small_call(proto_kernel, [arr(8, NX * COLS)], "proto_grad", at, *args)[0]


def small_call(kernel, outs, name, at, *args):
    whole = lambda v: pl.BlockSpec(v.shape, lambda i, at, n=len(v.shape): (0,) * n)
    return pl.pallas_call(
        kernel,
        grid_spec=pltpu.PrefetchScalarGridSpec(
            num_scalar_prefetch=1,
            grid=(1,),
            in_specs=[whole(v) for v in args],
            out_specs=[whole(v) for v in outs],
        ),
        out_shape=outs,
        cost_estimate=cost(1),
        compiler_params=pltpu.CompilerParams(vmem_limit_bytes=6 * MIB),
        name=name,
    )(at, *args)


def shift(v, axis, size, d):
    return lax.ppermute(v, axis, [(i, (i + d) % size) for i in range(size)])


def exchange(v, axes):
    return lax.all_to_all(v, axes, 0, 0, tiled=False)


def shards(teacher_feat, student_feat, teacher_weight, student_weight, crop_to_image):
    ix, iz = lax.axis_index("x"), lax.axis_index("z")
    iy, ic = lax.axis_index("y"), lax.axis_index("c")
    at = jnp.stack([ix, ic, iz, iy]).astype(jnp.int32)
    group = ("x", "y", "c")
    together = lax.optimization_barrier

    tf_all = jnp.broadcast_to(teacher_feat.astype(f32)[None], (NX, TB_DEV, K))
    tf_all = exchange(tf_all, ("x",))
    rows = SB_DEV // NC
    crops = jnp.pad(crop_to_image.astype(f32).reshape(NC, rows), ((0, 6), (0, K - rows)))
    own, half = pack_pass(at, student_feat, crops)
    mine = [shift(half, "x", NX, d) for d in (1, 3, 2)]
    share = (K, COLS)
    tn, tv = norm_pass(
        at, teacher_weight, [pltpu.HBM(share, bf16), pltpu.VMEM(share, bf16)], "teacher_norm"
    )
    tf_all, tn, tv, own = together((tf_all, tn, tv, own))

    c_parts, tu = teacher_pass(tf_all, tv)
    r_parts = row_pass(exchange(c_parts, ("z",)), tu, tv)[0]
    r_parts, at_1 = together((r_parts, at))
    r_parts = exchange(r_parts, group)
    (sn,) = norm_pass(at_1, student_weight, [pltpu.HBM(share, bf16)], "student_norm")
    c_parts, sn, *mine = together((col_pass(r_parts, tu, tv), sn, *mine))
    c_parts = exchange(c_parts, ("z",))
    core = [shift(v, "c", NC, 1) for v in mine]
    c_parts, *core = together((c_parts, *core))
    r_parts, tu = together((row_pass(c_parts, tu, tv)[0], tu))
    r_parts = exchange(r_parts, group)
    mine, core = (mine[0], mine[2], mine[1]), (core[0], core[2], core[1])
    ub, ubt, ut, tuc, crops, mine = rows_pass(at, own, mine, core, tu)
    r_parts, ub, ubt, ut, tuc = together((r_parts, ub, ubt, ut, tuc))
    c_parts, ub = together((col_pass(r_parts, tu, tv), ub))
    c_parts = exchange(c_parts, ("z",))
    sums = student_pass(ub, sn)
    b, parts = row_pass(c_parts, tu, tv, sums)
    parts = exchange(parts, group)

    common = (ub, ubt, tuc, b, sn, tn)
    p0, g, coef = first_pass(at, crops, parts, *common)
    up = lambda v: shift(v, "z", NZ, 1)
    down = lambda v: shift(v, "z", NZ, -1)
    u0, d0 = up(p0[4]), down(p0[5])
    p1, g = second_pass(at, coef, g, ut, *common)
    u0, d0, g, *p1 = together((u0, d0, g, *p1))
    g = exchange(g, group)
    u1, d1 = up(p1[3]), down(p1[4])
    for k in (3, 2):
        u0, d0 = up(u0 + p0[k]), down(d0 + p0[9 - k])
        u1, d1 = up(u1 + p1[k - 1]), down(d1 + p1[8 - k])
    u0, d1 = up(u0 + p0[1]), down(d1 + p1[7])
    own, *give = merge_pass(at, p0[0], u0, d0, p1[0], u1, d1)
    got = [shift(v, "x", NX, d) for v, d in zip(give, (1, 2, 3))]
    proto_grad = proto_pass(at, own, *got)
    feat_grad = feat_pass(g, mine).T
    return (feat_grad, proto_grad)


def solution(mesh):
    split = Mesh(mesh.devices.reshape(NX, NZ, NY, NC), ("x", "z", "y", "c"))
    dp, mp = ("x", "z"), ("y", "c")
    return jax.shard_map(
        shards,
        mesh=split,
        in_specs=(P(dp, None), P(dp, None), P(None, mp), P(None, mp), P(dp)),
        out_specs=(P(dp, mp), P(dp, mp)),
        check_vma=False,
    )
```

```python
import functools

import jax
import jax.numpy as jnp
from jax import lax
from jax.experimental import pallas as pl
from jax.experimental.pallas import tpu as pltpu
from jax.sharding import Mesh
from jax.sharding import PartitionSpec as P

K = 256
P_SIZE = 65536
TB_DEV = 96
TB_TOTAL = 3072
ITERS = 3
SB_DEV = 480
NX, NZ, NY, NC = 4, 8, 4, 2
NROW = NX * NY * NC
COLS = P_SIZE // NROW
LG = COLS // 128
TROWS = NX * TB_DEV
SROWS = NX * SB_DEV

eps = 1e-06
t_temp = 0.07
s_temp = 0.1
loss_scale = 1024.0

f32 = jnp.float32
bf16 = jnp.bfloat16
MIB = 1024 * 1024
GRAD_MIB = 28
LOG2E = 1.4426950408889634
HALF = COLS // 2


def unit_scale(v):
    return lax.rsqrt(jnp.sum(v * v, axis=1, keepdims=True) + eps)


def norm_columns(w):
    v = w.astype(f32)
    return (v * lax.rsqrt(jnp.sum(v * v, axis=0, keepdims=True) + eps)).astype(bf16)


def dot(a, b, ca, cb):
    return lax.dot_general(a, b, (((ca,), (cb,)), ((), ())), preferred_element_type=f32)


def lane_groups(v):
    return jnp.concatenate([v[:, 128 * k : 128 * (k + 1)] for k in range(v.shape[1] // 128)], 0)


def in_hbm(v):
    return pltpu.with_memory_space_constraint(v, pltpu.HBM)


def in_vmem(v):
    return pltpu.with_memory_space_constraint(v, pltpu.VMEM)


def cost(us):
    return pl.CostEstimate(flops=int(us * 1e9), bytes_accessed=0, transcendentals=0)


def call(kernel, out_shape, name, mib, scratch=(), us=1):
    return pl.pallas_call(
        kernel,
        out_shape=out_shape,
        cost_estimate=cost(us),
        scratch_shapes=list(scratch),
        compiler_params=pltpu.CompilerParams(vmem_limit_bytes=mib * MIB),
        name=name,
    )


def arr(*shape, dtype=f32):
    return jax.ShapeDtypeStruct(shape, dtype)


def norm_kernel(at, w, *outs):
    n = norm_columns(w[...])
    for out in outs:
        out[...] = n


def norm_pass(at, w, outs, name):
    return pl.pallas_call(
        norm_kernel,
        grid_spec=pltpu.PrefetchScalarGridSpec(
            num_scalar_prefetch=1,
            grid=(2,),
            in_specs=[pl.BlockSpec((K, 1024), lambda j, at: (0, at[0] * 2 + j))],
            out_specs=[pl.BlockSpec((K, 1024), lambda j, at: (0, j))] * len(outs),
        ),
        out_shape=outs,
        cost_estimate=cost(2),
        compiler_params=pltpu.CompilerParams(vmem_limit_bytes=12 * MIB),
        name=name,
    )(at, in_hbm(w))


def pack_kernel(at, sf, crops, own, half):
    n = SB_DEV // NC
    own[:SB_DEV, :] = sf[...].astype(f32)
    own[SB_DEV:, :] = crops[...]
    half[:n, :] = own[pl.ds(pl.multiple_of(at[1] * n, 8), n), :]
    row = jnp.where(at[1] == 0, crops[0:1, :], crops[1:2, :])
    half[n:, :] = jnp.broadcast_to(row, (8, K))


def pack_pass(at, sf, crops):
    outs = [pltpu.HBM((SB_DEV + 8, K), f32), pltpu.HBM((SB_DEV // NC + 8, K), f32)]
    return small_call(pack_kernel, outs, "pack_rows", at, sf, crops)


def exponentials(tu, tn, j):
    return jnp.exp2(dot(tu[...], tn[:, 512 * j : 512 * (j + 1)], 1, 0) * (LOG2E / t_temp))


def put_columns(c_out, j, c):
    for k in range(4):
        part = c[None, :, 128 * k : 128 * (k + 1)]
        c_out[:, 4 * j + k : 4 * j + k + 1, :] = jnp.broadcast_to(part, (NZ, 1, 128))


def teacher_kernel(tf, tn, c_out, tu_out):
    for x in range(NX):
        v = tf[x]
        tu_out[x * TB_DEV : (x + 1) * TB_DEV, :] = (v * unit_scale(v)).astype(bf16)
    for j in range(COLS // 512):
        put_columns(c_out, j, jnp.sum(exponentials(tu_out, tn, j), axis=0, keepdims=True))


def teacher_pass(tf_all, tn):
    outs = [arr(NZ, LG, 128), pltpu.VMEM((TROWS, K), bf16)]
    return call(teacher_kernel, outs, "teacher_scores", 12)(tf_all, in_vmem(tn))


def row_kernel(tail, c_parts, tu, tn, *refs):
    if tail:
        extra, b_out, r_out = refs
        r_out[:, 8:, :] = jnp.broadcast_to(extra[...][None], (NROW, 16, 128))
    else:
        (r_out,) = refs
    b = 1.0 / (jnp.sum(c_parts[...], axis=0) * P_SIZE)
    if tail:
        b_out[...] = b
    acc = None
    for j in range(COLS // 512):
        e = exponentials(tu, tn, j)
        for k in range(4):
            part = e[:, 128 * k : 128 * (k + 1)] * b[4 * j + k : 4 * j + k + 1, :]
            acc = part if acc is None else acc + part
    r = [jnp.sum(acc[128 * k : 128 * (k + 1), :].T, axis=0, keepdims=True) for k in range(3)]
    r = jnp.concatenate(r + [jnp.ones((5, 128), f32)], 0)
    r_out[:, :8, :] = jnp.broadcast_to(r[None], (NROW, 8, 128))


def row_pass(c_parts, tu, tn, *extra):
    tail = len(extra) > 0
    outs = [arr(LG, 128), arr(NROW, 24, 128)] if tail else [arr(NROW, 8, 128)]
    name = "last_row_sums" if tail else "row_sums"
    kernel = functools.partial(row_kernel, tail)
    return call(kernel, outs, name, 12)(c_parts, in_vmem(tu), in_vmem(tn), *extra)


def col_kernel(r_parts, tu, tn, c_out):
    a = 1.0 / (jnp.sum(r_parts[...], axis=0) * TB_TOTAL)
    wide = jnp.concatenate([jnp.broadcast_to(a[k : k + 1, :], (128, 128)).T for k in range(3)], 0)
    wide = jnp.concatenate([wide] * 4, 1)
    for j in range(COLS // 512):
        put_columns(c_out, j, jnp.sum(exponentials(tu, tn, j) * wide, axis=0, keepdims=True))


def col_pass(r_parts, tu, tn):
    return call(col_kernel, arr(NZ, LG, 128), "col_sums", 12)(r_parts, in_vmem(tu), in_vmem(tn))


def rows_kernel(at, own, mine_1, mine_2, mine_3, core_1, core_2, core_3, tu, *refs):
    ub_out, ubt_out, ut_out, tuc_out, crop_out, mine_out, sf = refs
    ix, ic = at[0], at[1]
    half = SB_DEV // NC
    spare = jnp.zeros((1, 512 - SB_DEV), f32)
    crop_out[...] = jnp.zeros_like(crop_out)
    sf[ix] = own[:SB_DEV, :]
    row = jnp.concatenate([own[SB_DEV : SB_DEV + 1, :half], own[SB_DEV + 1 : SB_DEV + 2, :half], spare], 1)
    crop_out[ix, 0:1, :] = row
    for d, mine, core in ((1, mine_1, core_1), (2, mine_2, core_2), (3, mine_3, core_3)):
        x = lax.rem(ix + NX - d, NX)
        sf[x, pl.ds(pl.multiple_of(ic * half, 8), half), :] = mine[:half, :]
        sf[x, pl.ds(pl.multiple_of((1 - ic) * half, 8), half), :] = core[:half, :]
        m, c = mine[half : half + 1, :half], core[half : half + 1, :half]
        row = jnp.concatenate([jnp.where(ic == 0, m, c), jnp.where(ic == 0, c, m), spare], 1)
        crop_out[x, 0:1, :] = row
    for x in range(NX):
        rows = slice(x * SB_DEV, (x + 1) * SB_DEV)
        v = sf[x]
        scale = unit_scale(v)
        u = v * scale
        ub_out[rows, :] = u.astype(bf16)
        crop_out[x, 1:2, :SB_DEV] = jnp.broadcast_to(scale, (SB_DEV, 128)).T[0:1, :]
        ut = u.T
        ut_out[x] = ut
        ubt_out[x] = ut.astype(bf16)
        row = lax.broadcasted_iota(jnp.int32, (TB_DEV, SB_DEV), 0)
        pick = row == crop_out[x, 0:1, :SB_DEV].astype(jnp.int32)
        pick = jnp.where(pick, 1.0, 0.0).astype(bf16)
        tuc_out[rows, :] = dot(pick, tu[x * TB_DEV : (x + 1) * TB_DEV, :], 0, 0).astype(bf16)
    mine_out[:32, :] = ut_out[ix, pl.ds(pl.multiple_of((at[3] * NC + ic) * 32, 8), 32), :]
    mine_out[32:, :] = jnp.broadcast_to(crop_out[ix, 1:2, :SB_DEV], (8, SB_DEV))


def rows_pass(at, own, mine, core, tu):
    whole = lambda shape: pl.BlockSpec(shape, lambda i, at: (0,) * len(shape))
    half = whole((SB_DEV // NC + 8, K))
    outs = [
        arr(SROWS, K, dtype=bf16),
        arr(NX, K, SB_DEV, dtype=bf16),
        arr(NX, K, SB_DEV),
        arr(SROWS, K, dtype=bf16),
        arr(NX, 8, 512),
        arr(40, SB_DEV),
    ]
    return pl.pallas_call(
        rows_kernel,
        grid_spec=pltpu.PrefetchScalarGridSpec(
            num_scalar_prefetch=1,
            grid=(1,),
            in_specs=[whole((SB_DEV + 8, K))] + [half] * 6 + [whole((TROWS, K))],
            out_specs=[whole(v.shape) for v in outs],
            scratch_shapes=[pltpu.VMEM((NX, SB_DEV, K), f32)],
        ),
        out_shape=[pltpu.HBM(v.shape, v.dtype) for v in outs],
        cost_estimate=cost(3),
        compiler_params=pltpu.CompilerParams(vmem_limit_bytes=20 * MIB),
        name="student_units",
    )(at, *[in_hbm(v) for v in (own, *mine, *core)], tu)


def student_kernel(ub, sn, rs_out):
    @pl.loop(0, NX)
    def _(x):
        rows = pl.ds(pl.multiple_of(x * SB_DEV, 32), SB_DEV)
        total = None
        for j in range(COLS // 512):
            e = jnp.exp2(dot(ub[rows, :], sn[:, 512 * j : 512 * (j + 1)], 1, 0) * (LOG2E / s_temp))
            for k in range(4):
                part = e[:, 128 * k : 128 * (k + 1)]
                total = part if total is None else total + part
        for k in range(4):
            part = total[128 * k : min(128 * (k + 1), SB_DEV), :].T
            part = jnp.sum(part, axis=0, keepdims=True)
            if part.shape[1] < 128:
                part = jnp.concatenate([part, jnp.ones((1, 128 - part.shape[1]), f32)], 1)
            rs_out[pl.ds(4 * x + k, 1), :] = part


def student_pass(ub, sn):
    return call(student_kernel, arr(16, 128), "student_sums", 14, us=3)(ub, sn)


def factors(crops, parts, coef):
    total = jnp.sum(parts[...], axis=0)
    a = (loss_scale / s_temp) / total[:3]
    a = jnp.concatenate([a[0:1], a[1:2], a[2:3]], 1)
    s = (loss_scale / s_temp) / total[8:]
    row = lax.broadcasted_iota(jnp.int32, (TB_DEV, SB_DEV), 0)
    lane = lax.broadcasted_iota(jnp.int32, (128, 128), 1)
    for x in range(NX):
        ax = jnp.concatenate([a[:, x * TB_DEV : (x + 1) * TB_DEV], jnp.zeros((1, 32), f32)], 1)
        ax = jnp.broadcast_to(ax, (128, 128)).T[:TB_DEV, 0:1]
        pick = row == crops[x, 0:1, :SB_DEV].astype(jnp.int32)
        ac = jnp.sum(jnp.where(pick, ax, 0.0), axis=0, keepdims=True)
        ac = jnp.concatenate([ac, jnp.zeros((1, 512 - SB_DEV), f32)], 1)
        for k in range(4):
            ak = jnp.broadcast_to(ac[:, 128 * k : 128 * (k + 1)], (128, 128)).T
            sk = jnp.broadcast_to(s[4 * x + k : 4 * x + k + 1, :], (128, 128)).T
            n = min(128, SB_DEV - 128 * k)
            both = jnp.where(lane == 0, ak, sk)
            coef[x * SB_DEV + 128 * k : x * SB_DEV + 128 * k + n, :] = both[:n]


def grad_half(h, iz, ub, ubt, tuc, coef, b, sn, tn, p, p_outs, take):
    cols = slice(h * HALF, (h + 1) * HALF)
    bh = jnp.concatenate([b[k : k + 1, :] for k in range(h * LG // 2, (h + 1) * LG // 2)], 1)
    for x in range(NX):
        rows = slice(x * SB_DEV, (x + 1) * SB_DEV)
        q = jnp.exp2(dot(ub[rows, :], sn[:, cols], 1, 0) * (LOG2E / s_temp)) * coef[rows, 1:2]
        t = jnp.exp2(dot(tuc[rows, :], tn[:, cols], 1, 0) * (LOG2E / t_temp)) * bh
        d = (q - t * coef[rows, 0:1]).astype(bf16)
        prod = dot(ubt[x], d, 1, 0)
        if x == 0:
            p[...] = prod
        else:
            p[...] += prod
        take(x, rows, dot(d, sn[:, cols], 1, 1))
    for d in range(NZ):
        z = lax.rem(iz + d, NZ)
        for x in range(NX):
            p_outs[d][x] = p[pl.ds(pl.multiple_of(x * 64 + z * 8, 8), 8), :]


def first_kernel(at, crops, parts, ub, ubt, tuc, b, sn, tn, *refs):
    *p_outs, g_out, coef, p = refs
    factors(crops, parts, coef)

    def take(x, rows, part):
        g_out[rows, :] = part

    grad_half(0, at[2], ub, ubt, tuc, coef, b, sn, tn, p, p_outs, take)


def second_kernel(at, coef, g_in, ut, ub, ubt, tuc, b, sn, tn, *refs):
    *p_outs, g_out, p, g, sems = refs
    n, spare = NY * NC, SB_DEV // 32
    out = lambda x: pltpu.make_async_copy(g.at[x], g_out.at[pl.ds(x * n, n)], sems.at[x])

    def take(x, rows, part):
        gt = (g_in[rows, :] + part).T
        along = jnp.sum(ut[x] * gt, axis=0, keepdims=True)
        along = [along[:, 32 * i : 32 * (i + 1)] for i in range(spare)]
        along = jnp.concatenate(along + [jnp.zeros((32 - spare, 32), f32)], 0)
        for m in range(n):
            g[x, m] = jnp.concatenate([gt[32 * m : 32 * (m + 1), :], along], 1)
        out(x).start()

    grad_half(1, at[2], ub, ubt, tuc, coef, b, sn, tn, p, p_outs, take)
    for x in range(NX):
        out(x).wait()


def grad_call(kernel, outs, specs, name, scratch, at, *args):
    whole = lambda v: pl.BlockSpec(v.shape, lambda i, at, n=len(v.shape): (0,) * n)
    return pl.pallas_call(
        kernel,
        grid_spec=pltpu.PrefetchScalarGridSpec(
            num_scalar_prefetch=1,
            grid=(1,),
            in_specs=[whole(v) for v in args],
            out_specs=[whole(arr(NX, 8, HALF))] * NZ + (specs or [whole(v) for v in outs]),
            scratch_shapes=[pltpu.VMEM((K, HALF), f32)] + scratch,
        ),
        out_shape=[pltpu.HBM((NX, 8, HALF), f32)] * NZ + outs,
        cost_estimate=cost(8),
        compiler_params=pltpu.CompilerParams(vmem_limit_bytes=GRAD_MIB * MIB),
        name=name,
    )(at, *args)


def first_pass(at, crops, parts, *common):
    outs = [arr(SROWS, K), arr(SROWS, 128)]
    *p, g, coef = grad_call(first_kernel, outs, None, "first_half", [], at, crops, parts, *common)
    return p, g, coef


def second_pass(at, coef, g, ut, *common):
    outs, specs = [pltpu.HBM((NROW, 32, 512), f32)], [pl.BlockSpec(memory_space=pltpu.HBM)]
    scratch = [pltpu.VMEM((NX, NY * NC, 32, 512), f32), pltpu.SemaphoreType.DMA((NX,))]
    *p, g = grad_call(second_kernel, outs, specs, "second_half", scratch, at, coef, g, ut, *common)
    return p, g


def feat_kernel(parts, mine, out):
    g = jnp.sum(parts[...], axis=0)
    along = jnp.concatenate([g[i : i + 1, SB_DEV:] for i in range(SB_DEV // 32)], 1)
    out[...] = (g[:, :SB_DEV] - mine[:32, :] * along) * mine[32:33, :]


def feat_pass(parts, mine):
    return call(feat_kernel, arr(32, SB_DEV), "feat_grad", 8)(parts, mine)


def merge_kernel(at, p0, u0, d0, p1, u1, d1, *outs):
    for d in range(NX):
        x = lax.rem(at[0] + d, NX)
        outs[d][:, :HALF] = p0[x] + u0[x] + d0[x]
        outs[d][:, HALF:] = p1[x] + u1[x] + d1[x]


def merge_pass(at, *args):
    return small_call(merge_kernel, [arr(8, COLS)] * NX, "merge_sums", at, *args)


def proto_kernel(at, *refs):
    out = refs[NX]
    for d in range(NX):
        x = lax.rem(at[0] + NX - d, NX)
        out[:, pl.ds(pl.multiple_of(x * COLS, 128), COLS)] = refs[d][...]


def proto_pass(at, *args):
    return small_call(proto_kernel, [arr(8, NX * COLS)], "proto_grad", at, *args)[0]


def small_call(kernel, outs, name, at, *args):
    whole = lambda v: pl.BlockSpec(v.shape, lambda i, at, n=len(v.shape): (0,) * n)
    return pl.pallas_call(
        kernel,
        grid_spec=pltpu.PrefetchScalarGridSpec(
            num_scalar_prefetch=1,
            grid=(1,),
            in_specs=[whole(v) for v in args],
            out_specs=[whole(v) for v in outs],
        ),
        out_shape=outs,
        cost_estimate=cost(1),
        compiler_params=pltpu.CompilerParams(vmem_limit_bytes=6 * MIB),
        name=name,
    )(at, *args)


def shift(v, axis, size, d):
    return lax.ppermute(v, axis, [(i, (i + d) % size) for i in range(size)])


def exchange(v, axes):
    return lax.all_to_all(v, axes, 0, 0, tiled=False)


def shards(teacher_feat, student_feat, teacher_weight, student_weight, crop_to_image):
    ix, iz = lax.axis_index("x"), lax.axis_index("z")
    iy, ic = lax.axis_index("y"), lax.axis_index("c")
    at = jnp.stack([ix, ic, iz, iy]).astype(jnp.int32)
    group = ("x", "y", "c")
    together = lax.optimization_barrier

    tf_all = jnp.broadcast_to(teacher_feat.astype(f32)[None], (NX, TB_DEV, K))
    tf_all = exchange(tf_all, ("x",))
    rows = SB_DEV // NC
    crops = jnp.pad(crop_to_image.astype(f32).reshape(NC, rows), ((0, 6), (0, K - rows)))
    own, half = pack_pass(at, student_feat, crops)
    mine = [shift(half, "x", NX, d) for d in (1, 3, 2)]
    share = (K, COLS)
    tn, tv = norm_pass(
        at, teacher_weight, [pltpu.HBM(share, bf16), pltpu.VMEM(share, bf16)], "teacher_norm"
    )
    tf_all, tn, tv, own = together((tf_all, tn, tv, own))

    c_parts, tu = teacher_pass(tf_all, tv)
    r_parts = row_pass(exchange(c_parts, ("z",)), tu, tv)[0]
    r_parts, at_1 = together((r_parts, at))
    r_parts = exchange(r_parts, group)
    (sn,) = norm_pass(at_1, student_weight, [pltpu.HBM(share, bf16)], "student_norm")
    c_parts, sn, *mine = together((col_pass(r_parts, tu, tv), sn, *mine))
    c_parts = exchange(c_parts, ("z",))
    core = [shift(v, "c", NC, 1) for v in mine]
    c_parts, *core = together((c_parts, *core))
    r_parts, tu = together((row_pass(c_parts, tu, tv)[0], tu))
    r_parts = exchange(r_parts, group)
    mine, core = (mine[0], mine[2], mine[1]), (core[0], core[2], core[1])
    ub, ubt, ut, tuc, crops, mine = rows_pass(at, own, mine, core, tu)
    r_parts, ub, ubt, ut, tuc = together((r_parts, ub, ubt, ut, tuc))
    c_parts, ub = together((col_pass(r_parts, tu, tv), ub))
    c_parts = exchange(c_parts, ("z",))
    sums = student_pass(ub, sn)
    b, parts = row_pass(c_parts, tu, tv, sums)
    parts = exchange(parts, group)

    common = (ub, ubt, tuc, b, sn, tn)
    p0, g, coef = first_pass(at, crops, parts, *common)
    up = lambda v: shift(v, "z", NZ, 1)
    down = lambda v: shift(v, "z", NZ, -1)
    u0, d0 = up(p0[4]), down(p0[5])
    p1, g = second_pass(at, coef, g, ut, *common)
    u0, d0, g, *p1 = together((u0, d0, g, *p1))
    g = exchange(g, group)
    u1, d1 = up(p1[3]), down(p1[4])
    for k in (3, 2):
        u0, d0 = up(u0 + p0[k]), down(d0 + p0[9 - k])
        u1, d1 = up(u1 + p1[k - 1]), down(d1 + p1[8 - k])
    u0, d1 = up(u0 + p0[1]), down(d1 + p1[7])
    own, *give = merge_pass(at, p0[0], u0, d0, p1[0], u1, d1)
    got = [shift(v, "x", NX, d) for v, d in zip(give, (1, 2, 3))]
    proto_grad = proto_pass(at, own, *got)
    feat_grad = feat_pass(g, mine).T
    return (feat_grad, proto_grad)


def solution(mesh):
    split = Mesh(mesh.devices.reshape(NX, NZ, NY, NC), ("x", "z", "y", "c"))
    dp, mp = ("x", "z"), ("y", "c")
    return jax.shard_map(
        shards,
        mesh=split,
        in_specs=(P(dp, None), P(dp, None), P(None, mp), P(None, mp), P(dp)),
        out_specs=(P(dp, mp), P(dp, mp)),
        check_vma=False,
    )
```

```python
import functools

import jax
import jax.numpy as jnp
from jax import lax
from jax.experimental import pallas as pl
from jax.experimental.pallas import tpu as pltpu
from jax.sharding import Mesh
from jax.sharding import PartitionSpec as P

K = 256
P_SIZE = 65536
TB_DEV = 96
TB_TOTAL = 3072
ITERS = 3
SB_DEV = 480
NX, NZ, NY, NC = 4, 8, 4, 2
NROW = NX * NY * NC
COLS = P_SIZE // NROW
LG = COLS // 128
TROWS = NX * TB_DEV
SROWS = NX * SB_DEV

eps = 1e-06
t_temp = 0.07
s_temp = 0.1
loss_scale = 1024.0

f32 = jnp.float32
bf16 = jnp.bfloat16
MIB = 1024 * 1024
GRAD_MIB = 28
LOG2E = 1.4426950408889634
HALF = COLS // 2


def unit_scale(v):
    return lax.rsqrt(jnp.sum(v * v, axis=1, keepdims=True) + eps)


def norm_columns(w):
    v = w.astype(f32)
    return (v * lax.rsqrt(jnp.sum(v * v, axis=0, keepdims=True) + eps)).astype(bf16)


def dot(a, b, ca, cb):
    return lax.dot_general(a, b, (((ca,), (cb,)), ((), ())), preferred_element_type=f32)


def lane_groups(v):
    return jnp.concatenate([v[:, 128 * k : 128 * (k + 1)] for k in range(v.shape[1] // 128)], 0)


def in_hbm(v):
    return pltpu.with_memory_space_constraint(v, pltpu.HBM)


def in_vmem(v):
    return pltpu.with_memory_space_constraint(v, pltpu.VMEM)


def cost(us):
    return pl.CostEstimate(flops=int(us * 1e9), bytes_accessed=0, transcendentals=0)


def call(kernel, out_shape, name, mib, scratch=(), us=1):
    return pl.pallas_call(
        kernel,
        out_shape=out_shape,
        cost_estimate=cost(us),
        scratch_shapes=list(scratch),
        compiler_params=pltpu.CompilerParams(vmem_limit_bytes=mib * MIB),
        name=name,
    )


def arr(*shape, dtype=f32):
    return jax.ShapeDtypeStruct(shape, dtype)


def norm_kernel(at, w, *outs):
    n = norm_columns(w[...])
    for out in outs:
        out[...] = n


def norm_pass(at, w, outs, name):
    return pl.pallas_call(
        norm_kernel,
        grid_spec=pltpu.PrefetchScalarGridSpec(
            num_scalar_prefetch=1,
            grid=(2,),
            in_specs=[pl.BlockSpec((K, 1024), lambda j, at: (0, at[0] * 2 + j))],
            out_specs=[pl.BlockSpec((K, 1024), lambda j, at: (0, j))] * len(outs),
        ),
        out_shape=outs,
        cost_estimate=cost(2),
        compiler_params=pltpu.CompilerParams(vmem_limit_bytes=12 * MIB),
        name=name,
    )(at, in_hbm(w))


def pack_kernel(at, sf, crops, own, half):
    n = SB_DEV // NC
    own[:SB_DEV, :] = sf[...].astype(f32)
    own[SB_DEV:, :] = crops[...]
    half[:n, :] = own[pl.ds(pl.multiple_of(at[1] * n, 8), n), :]
    row = jnp.where(at[1] == 0, crops[0:1, :], crops[1:2, :])
    half[n:, :] = jnp.broadcast_to(row, (8, K))


def pack_pass(at, sf, crops):
    outs = [pltpu.HBM((SB_DEV + 8, K), f32), pltpu.HBM((SB_DEV // NC + 8, K), f32)]
    return small_call(pack_kernel, outs, "pack_rows", at, sf, crops)


def exponentials(tu, tn, j):
    return jnp.exp2(dot(tu[...], tn[:, 512 * j : 512 * (j + 1)], 1, 0) * (LOG2E / t_temp))


def put_columns(c_out, j, c):
    for k in range(4):
        part = c[None, :, 128 * k : 128 * (k + 1)]
        c_out[:, 4 * j + k : 4 * j + k + 1, :] = jnp.broadcast_to(part, (NZ, 1, 128))


def teacher_kernel(tf, tn, c_out, tu_out):
    for x in range(NX):
        v = tf[x]
        tu_out[x * TB_DEV : (x + 1) * TB_DEV, :] = (v * unit_scale(v)).astype(bf16)
    for j in range(COLS // 512):
        put_columns(c_out, j, jnp.sum(exponentials(tu_out, tn, j), axis=0, keepdims=True))


def teacher_pass(tf_all, tn):
    outs = [arr(NZ, LG, 128), pltpu.VMEM((TROWS, K), bf16)]
    return call(teacher_kernel, outs, "teacher_scores", 12)(tf_all, in_vmem(tn))


def row_kernel(tail, c_parts, tu, tn, *refs):
    if tail:
        extra, b_out, r_out = refs
        r_out[:, 8:, :] = jnp.broadcast_to(extra[...][None], (NROW, 16, 128))
    else:
        (r_out,) = refs
    b = 1.0 / (jnp.sum(c_parts[...], axis=0) * P_SIZE)
    if tail:
        b_out[...] = b
    acc = None
    for j in range(COLS // 512):
        e = exponentials(tu, tn, j)
        for k in range(4):
            part = e[:, 128 * k : 128 * (k + 1)] * b[4 * j + k : 4 * j + k + 1, :]
            acc = part if acc is None else acc + part
    r = [jnp.sum(acc[128 * k : 128 * (k + 1), :].T, axis=0, keepdims=True) for k in range(3)]
    r = jnp.concatenate(r + [jnp.ones((5, 128), f32)], 0)
    r_out[:, :8, :] = jnp.broadcast_to(r[None], (NROW, 8, 128))


def row_pass(c_parts, tu, tn, *extra):
    tail = len(extra) > 0
    outs = [arr(LG, 128), arr(NROW, 24, 128)] if tail else [arr(NROW, 8, 128)]
    name = "last_row_sums" if tail else "row_sums"
    kernel = functools.partial(row_kernel, tail)
    return call(kernel, outs, name, 12)(c_parts, in_vmem(tu), in_vmem(tn), *extra)


def col_kernel(r_parts, tu, tn, c_out):
    a = 1.0 / (jnp.sum(r_parts[...], axis=0) * TB_TOTAL)
    wide = jnp.concatenate([jnp.broadcast_to(a[k : k + 1, :], (128, 128)).T for k in range(3)], 0)
    wide = jnp.concatenate([wide] * 4, 1)
    for j in range(COLS // 512):
        put_columns(c_out, j, jnp.sum(exponentials(tu, tn, j) * wide, axis=0, keepdims=True))


def col_pass(r_parts, tu, tn):
    return call(col_kernel, arr(NZ, LG, 128), "col_sums", 12)(r_parts, in_vmem(tu), in_vmem(tn))


def rows_kernel(at, own, mine_1, mine_2, mine_3, core_1, core_2, core_3, tu, *refs):
    ub_out, ubt_out, ut_out, tuc_out, crop_out, mine_out, sf = refs
    ix, ic = at[0], at[1]
    half = SB_DEV // NC
    spare = jnp.zeros((1, 512 - SB_DEV), f32)
    crop_out[...] = jnp.zeros_like(crop_out)
    sf[ix] = own[:SB_DEV, :]
    row = jnp.concatenate([own[SB_DEV : SB_DEV + 1, :half], own[SB_DEV + 1 : SB_DEV + 2, :half], spare], 1)
    crop_out[ix, 0:1, :] = row
    for d, mine, core in ((1, mine_1, core_1), (2, mine_2, core_2), (3, mine_3, core_3)):
        x = lax.rem(ix + NX - d, NX)
        sf[x, pl.ds(pl.multiple_of(ic * half, 8), half), :] = mine[:half, :]
        sf[x, pl.ds(pl.multiple_of((1 - ic) * half, 8), half), :] = core[:half, :]
        m, c = mine[half : half + 1, :half], core[half : half + 1, :half]
        row = jnp.concatenate([jnp.where(ic == 0, m, c), jnp.where(ic == 0, c, m), spare], 1)
        crop_out[x, 0:1, :] = row
    for x in range(NX):
        rows = slice(x * SB_DEV, (x + 1) * SB_DEV)
        v = sf[x]
        scale = unit_scale(v)
        u = v * scale
        ub_out[rows, :] = u.astype(bf16)
        crop_out[x, 1:2, :SB_DEV] = jnp.broadcast_to(scale, (SB_DEV, 128)).T[0:1, :]
        ut = u.T
        ut_out[x] = ut
        ubt_out[x] = ut.astype(bf16)
        row = lax.broadcasted_iota(jnp.int32, (TB_DEV, SB_DEV), 0)
        pick = row == crop_out[x, 0:1, :SB_DEV].astype(jnp.int32)
        pick = jnp.where(pick, 1.0, 0.0).astype(bf16)
        tuc_out[rows, :] = dot(pick, tu[x * TB_DEV : (x + 1) * TB_DEV, :], 0, 0).astype(bf16)
    mine_out[:32, :] = ut_out[ix, pl.ds(pl.multiple_of((at[3] * NC + ic) * 32, 8), 32), :]
    mine_out[32:, :] = jnp.broadcast_to(crop_out[ix, 1:2, :SB_DEV], (8, SB_DEV))


def rows_pass(at, own, mine, core, tu):
    whole = lambda shape: pl.BlockSpec(shape, lambda i, at: (0,) * len(shape))
    half = whole((SB_DEV // NC + 8, K))
    outs = [
        arr(SROWS, K, dtype=bf16),
        arr(NX, K, SB_DEV, dtype=bf16),
        arr(NX, K, SB_DEV),
        arr(SROWS, K, dtype=bf16),
        arr(NX, 8, 512),
        arr(40, SB_DEV),
    ]
    return pl.pallas_call(
        rows_kernel,
        grid_spec=pltpu.PrefetchScalarGridSpec(
            num_scalar_prefetch=1,
            grid=(1,),
            in_specs=[whole((SB_DEV + 8, K))] + [half] * 6 + [whole((TROWS, K))],
            out_specs=[whole(v.shape) for v in outs],
            scratch_shapes=[pltpu.VMEM((NX, SB_DEV, K), f32)],
        ),
        out_shape=[pltpu.HBM(v.shape, v.dtype) for v in outs],
        cost_estimate=cost(3),
        compiler_params=pltpu.CompilerParams(vmem_limit_bytes=20 * MIB),
        name="student_units",
    )(at, *[in_hbm(v) for v in (own, *mine, *core)], tu)


def student_kernel(ub, sn, rs_out):
    @pl.loop(0, NX)
    def _(x):
        rows = pl.ds(pl.multiple_of(x * SB_DEV, 32), SB_DEV)
        total = None
        for j in range(COLS // 512):
            e = jnp.exp2(dot(ub[rows, :], sn[:, 512 * j : 512 * (j + 1)], 1, 0) * (LOG2E / s_temp))
            for k in range(4):
                part = e[:, 128 * k : 128 * (k + 1)]
                total = part if total is None else total + part
        for k in range(4):
            part = total[128 * k : min(128 * (k + 1), SB_DEV), :].T
            part = jnp.sum(part, axis=0, keepdims=True)
            if part.shape[1] < 128:
                part = jnp.concatenate([part, jnp.ones((1, 128 - part.shape[1]), f32)], 1)
            rs_out[pl.ds(4 * x + k, 1), :] = part


def student_pass(ub, sn):
    return call(student_kernel, arr(16, 128), "student_sums", 14, us=3)(ub, sn)


def factors(crops, parts, coef):
    total = jnp.sum(parts[...], axis=0)
    a = (loss_scale / s_temp) / total[:3]
    a = jnp.concatenate([a[0:1], a[1:2], a[2:3]], 1)
    s = (loss_scale / s_temp) / total[8:]
    row = lax.broadcasted_iota(jnp.int32, (TB_DEV, SB_DEV), 0)
    lane = lax.broadcasted_iota(jnp.int32, (128, 128), 1)
    for x in range(NX):
        ax = jnp.concatenate([a[:, x * TB_DEV : (x + 1) * TB_DEV], jnp.zeros((1, 32), f32)], 1)
        ax = jnp.broadcast_to(ax, (128, 128)).T[:TB_DEV, 0:1]
        pick = row == crops[x, 0:1, :SB_DEV].astype(jnp.int32)
        ac = jnp.sum(jnp.where(pick, ax, 0.0), axis=0, keepdims=True)
        ac = jnp.concatenate([ac, jnp.zeros((1, 512 - SB_DEV), f32)], 1)
        for k in range(4):
            ak = jnp.broadcast_to(ac[:, 128 * k : 128 * (k + 1)], (128, 128)).T
            sk = jnp.broadcast_to(s[4 * x + k : 4 * x + k + 1, :], (128, 128)).T
            n = min(128, SB_DEV - 128 * k)
            both = jnp.where(lane == 0, ak, sk)
            coef[x * SB_DEV + 128 * k : x * SB_DEV + 128 * k + n, :] = both[:n]


def grad_half(h, iz, ub, ubt, tuc, coef, b, sn, tn, p, p_outs, take):
    cols = slice(h * HALF, (h + 1) * HALF)
    bh = jnp.concatenate([b[k : k + 1, :] for k in range(h * LG // 2, (h + 1) * LG // 2)], 1)
    for x in range(NX):
        rows = slice(x * SB_DEV, (x + 1) * SB_DEV)
        q = jnp.exp2(dot(ub[rows, :], sn[:, cols], 1, 0) * (LOG2E / s_temp)) * coef[rows, 1:2]
        t = jnp.exp2(dot(tuc[rows, :], tn[:, cols], 1, 0) * (LOG2E / t_temp)) * bh
        d = (q - t * coef[rows, 0:1]).astype(bf16)
        prod = dot(ubt[x], d, 1, 0)
        if x == 0:
            p[...] = prod
        else:
            p[...] += prod
        take(x, rows, dot(d, sn[:, cols], 1, 1))
    for d in range(NZ):
        z = lax.rem(iz + d, NZ)
        for x in range(NX):
            p_outs[d][x] = p[pl.ds(pl.multiple_of(x * 64 + z * 8, 8), 8), :]


def first_kernel(at, crops, parts, ub, ubt, tuc, b, sn, tn, *refs):
    *p_outs, g_out, coef, p = refs
    factors(crops, parts, coef)

    def take(x, rows, part):
        g_out[rows, :] = part

    grad_half(0, at[2], ub, ubt, tuc, coef, b, sn, tn, p, p_outs, take)


def second_kernel(at, coef, g_in, ut, ub, ubt, tuc, b, sn, tn, *refs):
    *p_outs, g_out, p, g, sems = refs
    n, spare = NY * NC, SB_DEV // 32
    out = lambda x: pltpu.make_async_copy(g.at[x], g_out.at[pl.ds(x * n, n)], sems.at[x])

    def take(x, rows, part):
        gt = (g_in[rows, :] + part).T
        along = jnp.sum(ut[x] * gt, axis=0, keepdims=True)
        along = [along[:, 32 * i : 32 * (i + 1)] for i in range(spare)]
        along = jnp.concatenate(along + [jnp.zeros((32 - spare, 32), f32)], 0)
        for m in range(n):
            g[x, m] = jnp.concatenate([gt[32 * m : 32 * (m + 1), :], along], 1)
        out(x).start()

    grad_half(1, at[2], ub, ubt, tuc, coef, b, sn, tn, p, p_outs, take)
    for x in range(NX):
        out(x).wait()


def grad_call(kernel, outs, specs, name, scratch, at, *args):
    whole = lambda v: pl.BlockSpec(v.shape, lambda i, at, n=len(v.shape): (0,) * n)
    return pl.pallas_call(
        kernel,
        grid_spec=pltpu.PrefetchScalarGridSpec(
            num_scalar_prefetch=1,
            grid=(1,),
            in_specs=[whole(v) for v in args],
            out_specs=[whole(arr(NX, 8, HALF))] * NZ + (specs or [whole(v) for v in outs]),
            scratch_shapes=[pltpu.VMEM((K, HALF), f32)] + scratch,
        ),
        out_shape=[pltpu.HBM((NX, 8, HALF), f32)] * NZ + outs,
        cost_estimate=cost(8),
        compiler_params=pltpu.CompilerParams(vmem_limit_bytes=GRAD_MIB * MIB),
        name=name,
    )(at, *args)


def first_pass(at, crops, parts, *common):
    outs = [arr(SROWS, K), arr(SROWS, 128)]
    *p, g, coef = grad_call(first_kernel, outs, None, "first_half", [], at, crops, parts, *common)
    return p, g, coef


def second_pass(at, coef, g, ut, *common):
    outs, specs = [pltpu.HBM((NROW, 32, 512), f32)], [pl.BlockSpec(memory_space=pltpu.HBM)]
    scratch = [pltpu.VMEM((NX, NY * NC, 32, 512), f32), pltpu.SemaphoreType.DMA((NX,))]
    *p, g = grad_call(second_kernel, outs, specs, "second_half", scratch, at, coef, g, ut, *common)
    return p, g


def feat_kernel(parts, mine, out):
    g = jnp.sum(parts[...], axis=0)
    along = jnp.concatenate([g[i : i + 1, SB_DEV:] for i in range(SB_DEV // 32)], 1)
    out[...] = (g[:, :SB_DEV] - mine[:32, :] * along) * mine[32:33, :]


def feat_pass(parts, mine):
    return call(feat_kernel, arr(32, SB_DEV), "feat_grad", 8)(parts, mine)


def merge_kernel(at, p0, u0, d0, p1, u1, d1, *outs):
    for d in range(NX):
        x = lax.rem(at[0] + d, NX)
        outs[d][:, :HALF] = p0[x] + u0[x] + d0[x]
        outs[d][:, HALF:] = p1[x] + u1[x] + d1[x]


def merge_pass(at, *args):
    return small_call(merge_kernel, [arr(8, COLS)] * NX, "merge_sums", at, *args)


def proto_kernel(at, *refs):
    out = refs[NX]
    for d in range(NX):
        x = lax.rem(at[0] + NX - d, NX)
        out[:, pl.ds(pl.multiple_of(x * COLS, 128), COLS)] = refs[d][...]


def proto_pass(at, *args):
    return small_call(proto_kernel, [arr(8, NX * COLS)], "proto_grad", at, *args)[0]


def small_call(kernel, outs, name, at, *args):
    whole = lambda v: pl.BlockSpec(v.shape, lambda i, at, n=len(v.shape): (0,) * n)
    return pl.pallas_call(
        kernel,
        grid_spec=pltpu.PrefetchScalarGridSpec(
            num_scalar_prefetch=1,
            grid=(1,),
            in_specs=[whole(v) for v in args],
            out_specs=[whole(v) for v in outs],
        ),
        out_shape=outs,
        cost_estimate=cost(1),
        compiler_params=pltpu.CompilerParams(vmem_limit_bytes=6 * MIB),
        name=name,
    )(at, *args)


def shift(v, axis, size, d):
    return lax.ppermute(v, axis, [(i, (i + d) % size) for i in range(size)])


def exchange(v, axes):
    return lax.all_to_all(v, axes, 0, 0, tiled=False)


def shards(teacher_feat, student_feat, teacher_weight, student_weight, crop_to_image):
    ix, iz = lax.axis_index("x"), lax.axis_index("z")
    iy, ic = lax.axis_index("y"), lax.axis_index("c")
    at = jnp.stack([ix, ic, iz, iy]).astype(jnp.int32)
    group = ("x", "y", "c")
    together = lax.optimization_barrier

    tf_all = jnp.broadcast_to(teacher_feat.astype(f32)[None], (NX, TB_DEV, K))
    tf_all = exchange(tf_all, ("x",))
    rows = SB_DEV // NC
    crops = jnp.pad(crop_to_image.astype(f32).reshape(NC, rows), ((0, 6), (0, K - rows)))
    own, half = pack_pass(at, student_feat, crops)
    mine = [shift(half, "x", NX, d) for d in (1, 3, 2)]
    share = (K, COLS)
    tn, tv = norm_pass(
        at, teacher_weight, [pltpu.HBM(share, bf16), pltpu.VMEM(share, bf16)], "teacher_norm"
    )
    tf_all, tn, tv, own = together((tf_all, tn, tv, own))

    c_parts, tu = teacher_pass(tf_all, tv)
    r_parts = row_pass(exchange(c_parts, ("z",)), tu, tv)[0]
    r_parts, at_1 = together((r_parts, at))
    r_parts = exchange(r_parts, group)
    (sn,) = norm_pass(at_1, student_weight, [pltpu.HBM(share, bf16)], "student_norm")
    c_parts, sn, *mine = together((col_pass(r_parts, tu, tv), sn, *mine))
    c_parts = exchange(c_parts, ("z",))
    core = [shift(v, "c", NC, 1) for v in mine]
    c_parts, *core = together((c_parts, *core))
    r_parts, tu = together((row_pass(c_parts, tu, tv)[0], tu))
    r_parts = exchange(r_parts, group)
    mine, core = (mine[0], mine[2], mine[1]), (core[0], core[2], core[1])
    ub, ubt, ut, tuc, crops, mine = rows_pass(at, own, mine, core, tu)
    r_parts, ub, ubt, ut, tuc = together((r_parts, ub, ubt, ut, tuc))
    c_parts, ub = together((col_pass(r_parts, tu, tv), ub))
    c_parts = exchange(c_parts, ("z",))
    sums = student_pass(ub, sn)
    b, parts = row_pass(c_parts, tu, tv, sums)
    parts = exchange(parts, group)

    common = (ub, ubt, tuc, b, sn, tn)
    p0, g, coef = first_pass(at, crops, parts, *common)
    up = lambda v: shift(v, "z", NZ, 1)
    down = lambda v: shift(v, "z", NZ, -1)
    u0, d0 = up(p0[4]), down(p0[5])
    p1, g = second_pass(at, coef, g, ut, *common)
    u0, d0, g, *p1 = together((u0, d0, g, *p1))
    g = exchange(g, group)
    u1, d1 = up(p1[3]), down(p1[4])
    for k in (3, 2):
        u0, d0 = up(u0 + p0[k]), down(d0 + p0[9 - k])
        u1, d1 = up(u1 + p1[k - 1]), down(d1 + p1[8 - k])
    u0, d1 = up(u0 + p0[1]), down(d1 + p1[7])
    own, *give = merge_pass(at, p0[0], u0, d0, p1[0], u1, d1)
    got = [shift(v, "x", NX, d) for v, d in zip(give, (1, 2, 3))]
    feat_grad = feat_pass(g, mine)
    feat_grad, *got = together((feat_grad, *got))
    proto_grad = proto_pass(at, own, *got)
    feat_grad = feat_grad.T
    return (feat_grad, proto_grad)


def solution(mesh):
    split = Mesh(mesh.devices.reshape(NX, NZ, NY, NC), ("x", "z", "y", "c"))
    dp, mp = ("x", "z"), ("y", "c")
    return jax.shard_map(
        shards,
        mesh=split,
        in_specs=(P(dp, None), P(dp, None), P(None, mp), P(None, mp), P(dp)),
        out_specs=(P(dp, mp), P(dp, mp)),
        check_vma=False,
    )
```

```python
import functools

import jax
import jax.numpy as jnp
from jax import lax
from jax.experimental import pallas as pl
from jax.experimental.pallas import tpu as pltpu
from jax.sharding import Mesh
from jax.sharding import PartitionSpec as P

K = 256
P_SIZE = 65536
TB_DEV = 96
TB_TOTAL = 3072
ITERS = 3
SB_DEV = 480
NX, NZ, NY, NC = 4, 8, 4, 2
NROW = NX * NY * NC
COLS = P_SIZE // NROW
LG = COLS // 128
TROWS = NX * TB_DEV
SROWS = NX * SB_DEV

eps = 1e-06
t_temp = 0.07
s_temp = 0.1
loss_scale = 1024.0

f32 = jnp.float32
bf16 = jnp.bfloat16
MIB = 1024 * 1024
GRAD_MIB = 28
LOG2E = 1.4426950408889634
HALF = COLS // 2


def unit_scale(v):
    return lax.rsqrt(jnp.sum(v * v, axis=1, keepdims=True) + eps)


def norm_columns(w):
    v = w.astype(f32)
    return (v * lax.rsqrt(jnp.sum(v * v, axis=0, keepdims=True) + eps)).astype(bf16)


def dot(a, b, ca, cb):
    return lax.dot_general(a, b, (((ca,), (cb,)), ((), ())), preferred_element_type=f32)


def lane_groups(v):
    return jnp.concatenate([v[:, 128 * k : 128 * (k + 1)] for k in range(v.shape[1] // 128)], 0)


def in_hbm(v):
    return pltpu.with_memory_space_constraint(v, pltpu.HBM)


def in_vmem(v):
    return pltpu.with_memory_space_constraint(v, pltpu.VMEM)


def cost(us):
    return pl.CostEstimate(flops=int(us * 1e9), bytes_accessed=0, transcendentals=0)


def call(kernel, out_shape, name, mib, scratch=(), us=1):
    return pl.pallas_call(
        kernel,
        out_shape=out_shape,
        cost_estimate=cost(us),
        scratch_shapes=list(scratch),
        compiler_params=pltpu.CompilerParams(vmem_limit_bytes=mib * MIB),
        name=name,
    )


def arr(*shape, dtype=f32):
    return jax.ShapeDtypeStruct(shape, dtype)


def norm_kernel(at, w, *outs):
    n = norm_columns(w[...])
    for out in outs:
        out[...] = n


def norm_pass(at, w, outs, name):
    return pl.pallas_call(
        norm_kernel,
        grid_spec=pltpu.PrefetchScalarGridSpec(
            num_scalar_prefetch=1,
            grid=(2,),
            in_specs=[pl.BlockSpec((K, 1024), lambda j, at: (0, at[0] * 2 + j))],
            out_specs=[pl.BlockSpec((K, 1024), lambda j, at: (0, j))] * len(outs),
        ),
        out_shape=outs,
        cost_estimate=cost(2),
        compiler_params=pltpu.CompilerParams(vmem_limit_bytes=12 * MIB),
        name=name,
    )(at, in_hbm(w))


def pack_kernel(at, sf, crops, own, half):
    n = SB_DEV // NC
    own[:SB_DEV, :] = sf[...].astype(f32)
    own[SB_DEV:, :] = crops[...]
    half[:n, :] = own[pl.ds(pl.multiple_of(at[1] * n, 8), n), :]
    row = jnp.where(at[1] == 0, crops[0:1, :], crops[1:2, :])
    half[n:, :] = jnp.broadcast_to(row, (8, K))


def pack_pass(at, sf, crops):
    outs = [pltpu.HBM((SB_DEV + 8, K), f32), pltpu.HBM((SB_DEV // NC + 8, K), f32)]
    return small_call(pack_kernel, outs, "pack_rows", at, sf, crops)


def exponentials(tu, tn, j):
    return jnp.exp2(dot(tu[...], tn[:, 512 * j : 512 * (j + 1)], 1, 0) * (LOG2E / t_temp))


def put_columns(c_out, j, c):
    for k in range(4):
        part = c[None, :, 128 * k : 128 * (k + 1)]
        c_out[:, 4 * j + k : 4 * j + k + 1, :] = jnp.broadcast_to(part, (NZ, 1, 128))


def teacher_kernel(tf, tn, c_out, tu_out):
    for x in range(NX):
        v = tf[x]
        tu_out[x * TB_DEV : (x + 1) * TB_DEV, :] = (v * unit_scale(v)).astype(bf16)
    for j in range(COLS // 512):
        put_columns(c_out, j, jnp.sum(exponentials(tu_out, tn, j), axis=0, keepdims=True))


def teacher_pass(tf_all, tn):
    outs = [arr(NZ, LG, 128), pltpu.VMEM((TROWS, K), bf16)]
    return call(teacher_kernel, outs, "teacher_scores", 12)(tf_all, in_vmem(tn))


def row_kernel(tail, c_parts, tu, tn, *refs):
    if tail:
        extra, b_out, r_out = refs
        r_out[:, 8:, :] = jnp.broadcast_to(extra[...][None], (NROW, 16, 128))
    else:
        (r_out,) = refs
    b = 1.0 / (jnp.sum(c_parts[...], axis=0) * P_SIZE)
    if tail:
        b_out[...] = b
    acc = None
    for j in range(COLS // 512):
        e = exponentials(tu, tn, j)
        for k in range(4):
            part = e[:, 128 * k : 128 * (k + 1)] * b[4 * j + k : 4 * j + k + 1, :]
            acc = part if acc is None else acc + part
    r = [jnp.sum(acc[128 * k : 128 * (k + 1), :].T, axis=0, keepdims=True) for k in range(3)]
    r = jnp.concatenate(r + [jnp.ones((5, 128), f32)], 0)
    r_out[:, :8, :] = jnp.broadcast_to(r[None], (NROW, 8, 128))


def row_pass(c_parts, tu, tn, *extra):
    tail = len(extra) > 0
    outs = [arr(LG, 128), arr(NROW, 24, 128)] if tail else [arr(NROW, 8, 128)]
    name = "last_row_sums" if tail else "row_sums"
    kernel = functools.partial(row_kernel, tail)
    return call(kernel, outs, name, 12)(c_parts, in_vmem(tu), in_vmem(tn), *extra)


def col_kernel(r_parts, tu, tn, c_out):
    a = 1.0 / (jnp.sum(r_parts[...], axis=0) * TB_TOTAL)
    wide = jnp.concatenate([jnp.broadcast_to(a[k : k + 1, :], (128, 128)).T for k in range(3)], 0)
    wide = jnp.concatenate([wide] * 4, 1)
    for j in range(COLS // 512):
        put_columns(c_out, j, jnp.sum(exponentials(tu, tn, j) * wide, axis=0, keepdims=True))


def col_pass(r_parts, tu, tn):
    return call(col_kernel, arr(NZ, LG, 128), "col_sums", 12)(r_parts, in_vmem(tu), in_vmem(tn))


def rows_kernel(at, own, mine_1, mine_2, mine_3, core_1, core_2, core_3, tu, *refs):
    ub_out, ubt_out, ut_out, tuc_out, crop_out, mine_out, sf = refs
    ix, ic = at[0], at[1]
    half = SB_DEV // NC
    spare = jnp.zeros((1, 512 - SB_DEV), f32)
    crop_out[...] = jnp.zeros_like(crop_out)
    sf[ix] = own[:SB_DEV, :]
    row = jnp.concatenate([own[SB_DEV : SB_DEV + 1, :half], own[SB_DEV + 1 : SB_DEV + 2, :half], spare], 1)
    crop_out[ix, 0:1, :] = row
    for d, mine, core in ((1, mine_1, core_1), (2, mine_2, core_2), (3, mine_3, core_3)):
        x = lax.rem(ix + NX - d, NX)
        sf[x, pl.ds(pl.multiple_of(ic * half, 8), half), :] = mine[:half, :]
        sf[x, pl.ds(pl.multiple_of((1 - ic) * half, 8), half), :] = core[:half, :]
        m, c = mine[half : half + 1, :half], core[half : half + 1, :half]
        row = jnp.concatenate([jnp.where(ic == 0, m, c), jnp.where(ic == 0, c, m), spare], 1)
        crop_out[x, 0:1, :] = row
    for x in range(NX):
        rows = slice(x * SB_DEV, (x + 1) * SB_DEV)
        v = sf[x]
        scale = unit_scale(v)
        u = v * scale
        ub_out[rows, :] = u.astype(bf16)
        crop_out[x, 1:2, :SB_DEV] = jnp.broadcast_to(scale, (SB_DEV, 128)).T[0:1, :]
        ut = u.T
        ut_out[x] = ut
        ubt_out[x] = ut.astype(bf16)
        row = lax.broadcasted_iota(jnp.int32, (TB_DEV, SB_DEV), 0)
        pick = row == crop_out[x, 0:1, :SB_DEV].astype(jnp.int32)
        pick = jnp.where(pick, 1.0, 0.0).astype(bf16)
        tuc_out[rows, :] = dot(pick, tu[x * TB_DEV : (x + 1) * TB_DEV, :], 0, 0).astype(bf16)
    mine_out[:32, :] = ut_out[ix, pl.ds(pl.multiple_of((at[3] * NC + ic) * 32, 8), 32), :]
    mine_out[32:, :] = jnp.broadcast_to(crop_out[ix, 1:2, :SB_DEV], (8, SB_DEV))


def rows_pass(at, own, mine, core, tu):
    whole = lambda shape: pl.BlockSpec(shape, lambda i, at: (0,) * len(shape))
    half = whole((SB_DEV // NC + 8, K))
    outs = [
        arr(SROWS, K, dtype=bf16),
        arr(NX, K, SB_DEV, dtype=bf16),
        arr(NX, K, SB_DEV),
        arr(SROWS, K, dtype=bf16),
        arr(NX, 8, 512),
        arr(40, SB_DEV),
    ]
    return pl.pallas_call(
        rows_kernel,
        grid_spec=pltpu.PrefetchScalarGridSpec(
            num_scalar_prefetch=1,
            grid=(1,),
            in_specs=[whole((SB_DEV + 8, K))] + [half] * 6 + [whole((TROWS, K))],
            out_specs=[whole(v.shape) for v in outs],
            scratch_shapes=[pltpu.VMEM((NX, SB_DEV, K), f32)],
        ),
        out_shape=[pltpu.HBM(v.shape, v.dtype) for v in outs],
        cost_estimate=cost(3),
        compiler_params=pltpu.CompilerParams(vmem_limit_bytes=20 * MIB),
        name="student_units",
    )(at, *[in_hbm(v) for v in (own, *mine, *core)], tu)


def student_kernel(ub, sn, rs_out):
    @pl.loop(0, NX)
    def _(x):
        rows = pl.ds(pl.multiple_of(x * SB_DEV, 32), SB_DEV)
        total = None
        for j in range(COLS // 512):
            e = jnp.exp2(dot(ub[rows, :], sn[:, 512 * j : 512 * (j + 1)], 1, 0) * (LOG2E / s_temp))
            for k in range(4):
                part = e[:, 128 * k : 128 * (k + 1)]
                total = part if total is None else total + part
        for k in range(4):
            part = total[128 * k : min(128 * (k + 1), SB_DEV), :].T
            part = jnp.sum(part, axis=0, keepdims=True)
            if part.shape[1] < 128:
                part = jnp.concatenate([part, jnp.ones((1, 128 - part.shape[1]), f32)], 1)
            rs_out[pl.ds(4 * x + k, 1), :] = part


def student_pass(ub, sn):
    return call(student_kernel, arr(16, 128), "student_sums", 14, us=3)(ub, sn)


def factors(crops, parts, coef):
    total = jnp.sum(parts[...], axis=0)
    a = (loss_scale / s_temp) / total[:3]
    a = jnp.concatenate([a[0:1], a[1:2], a[2:3]], 1)
    s = (loss_scale / s_temp) / total[8:]
    row = lax.broadcasted_iota(jnp.int32, (TB_DEV, SB_DEV), 0)
    lane = lax.broadcasted_iota(jnp.int32, (128, 128), 1)
    for x in range(NX):
        ax = jnp.concatenate([a[:, x * TB_DEV : (x + 1) * TB_DEV], jnp.zeros((1, 32), f32)], 1)
        ax = jnp.broadcast_to(ax, (128, 128)).T[:TB_DEV, 0:1]
        pick = row == crops[x, 0:1, :SB_DEV].astype(jnp.int32)
        ac = jnp.sum(jnp.where(pick, ax, 0.0), axis=0, keepdims=True)
        ac = jnp.concatenate([ac, jnp.zeros((1, 512 - SB_DEV), f32)], 1)
        for k in range(4):
            ak = jnp.broadcast_to(ac[:, 128 * k : 128 * (k + 1)], (128, 128)).T
            sk = jnp.broadcast_to(s[4 * x + k : 4 * x + k + 1, :], (128, 128)).T
            n = min(128, SB_DEV - 128 * k)
            both = jnp.where(lane == 0, ak, sk)
            coef[x * SB_DEV + 128 * k : x * SB_DEV + 128 * k + n, :] = both[:n]


def grad_half(h, iz, ub, ubt, tuc, coef, b, sn, tn, p, p_outs, take):
    cols = slice(h * HALF, (h + 1) * HALF)
    bh = jnp.concatenate([b[k : k + 1, :] for k in range(h * LG // 2, (h + 1) * LG // 2)], 1)
    for x in range(NX):
        rows = slice(x * SB_DEV, (x + 1) * SB_DEV)
        q = jnp.exp2(dot(ub[rows, :], sn[:, cols], 1, 0) * (LOG2E / s_temp)) * coef[rows, 1:2]
        t = jnp.exp2(dot(tuc[rows, :], tn[:, cols], 1, 0) * (LOG2E / t_temp)) * bh
        d = (q - t * coef[rows, 0:1]).astype(bf16)
        prod = dot(ubt[x], d, 1, 0)
        if x == 0:
            p[...] = prod
        else:
            p[...] += prod
        take(x, rows, dot(d, sn[:, cols], 1, 1))
    for d in range(NZ):
        z = lax.rem(iz + d, NZ)
        for x in range(NX):
            p_outs[d][x] = p[pl.ds(pl.multiple_of(x * 64 + z * 8, 8), 8), :]


def first_kernel(at, crops, parts, ub, ubt, tuc, b, sn, tn, *refs):
    *p_outs, g_out, coef, p = refs
    factors(crops, parts, coef)

    def take(x, rows, part):
        g_out[rows, :] = part

    grad_half(0, at[2], ub, ubt, tuc, coef, b, sn, tn, p, p_outs, take)


def second_kernel(at, coef, g_in, ut, ub, ubt, tuc, b, sn, tn, *refs):
    *p_outs, g_out, p, g, sems = refs
    n, spare = NY * NC, SB_DEV // 32
    out = lambda x: pltpu.make_async_copy(g.at[x], g_out.at[pl.ds(x * n, n)], sems.at[x])

    def take(x, rows, part):
        gt = (g_in[rows, :] + part).T
        along = jnp.sum(ut[x] * gt, axis=0, keepdims=True)
        along = [along[:, 32 * i : 32 * (i + 1)] for i in range(spare)]
        along = jnp.concatenate(along + [jnp.zeros((32 - spare, 32), f32)], 0)
        for m in range(n):
            g[x, m] = jnp.concatenate([gt[32 * m : 32 * (m + 1), :], along], 1)
        out(x).start()

    grad_half(1, at[2], ub, ubt, tuc, coef, b, sn, tn, p, p_outs, take)
    for x in range(NX):
        out(x).wait()


def grad_call(kernel, outs, specs, first, name, scratch, at, *args):
    whole = lambda v: pl.BlockSpec(v.shape, lambda i, at, n=len(v.shape): (0,) * n)
    return pl.pallas_call(
        kernel,
        grid_spec=pltpu.PrefetchScalarGridSpec(
            num_scalar_prefetch=1,
            grid=(1,),
            in_specs=[whole(v) for v in args],
            out_specs=[whole(arr(NX, 8, HALF))] * NZ + (specs or [whole(v) for v in outs]),
            scratch_shapes=[pltpu.VMEM((K, HALF), f32)] + scratch,
        ),
        out_shape=[
            arr(NX, 8, HALF) if d in first else pltpu.HBM((NX, 8, HALF), f32) for d in range(NZ)
        ]
        + outs,
        cost_estimate=cost(8),
        compiler_params=pltpu.CompilerParams(vmem_limit_bytes=GRAD_MIB * MIB),
        name=name,
    )(at, *args)


def first_pass(at, crops, parts, *common):
    outs = [arr(SROWS, K), arr(SROWS, 128)]
    *p, g, coef = grad_call(first_kernel, outs, None, (4, 5), "first_half", [], at, crops, parts, *common)
    return p, g, coef


def second_pass(at, coef, g, ut, *common):
    outs, specs = [pltpu.HBM((NROW, 32, 512), f32)], [pl.BlockSpec(memory_space=pltpu.HBM)]
    scratch = [pltpu.VMEM((NX, NY * NC, 32, 512), f32), pltpu.SemaphoreType.DMA((NX,))]
    *p, g = grad_call(second_kernel, outs, specs, (3, 4), "second_half", scratch, at, coef, g, ut, *common)
    return p, g


def feat_kernel(parts, mine, out):
    g = jnp.sum(parts[...], axis=0)
    along = jnp.concatenate([g[i : i + 1, SB_DEV:] for i in range(SB_DEV // 32)], 1)
    out[...] = (g[:, :SB_DEV] - mine[:32, :] * along) * mine[32:33, :]


def feat_pass(parts, mine):
    return call(feat_kernel, arr(32, SB_DEV), "feat_grad", 8)(parts, mine)


def merge_kernel(at, p0, u0, d0, p1, u1, d1, *outs):
    for d in range(NX):
        x = lax.rem(at[0] + d, NX)
        outs[d][:, :HALF] = p0[x] + u0[x] + d0[x]
        outs[d][:, HALF:] = p1[x] + u1[x] + d1[x]


def merge_pass(at, *args):
    return small_call(merge_kernel, [arr(8, COLS)] * NX, "merge_sums", at, *args)


def proto_kernel(at, *refs):
    out = refs[NX]
    for d in range(NX):
        x = lax.rem(at[0] + NX - d, NX)
        out[:, pl.ds(pl.multiple_of(x * COLS, 128), COLS)] = refs[d][...]


def proto_pass(at, *args):
    return small_call(proto_kernel, [arr(8, NX * COLS)], "proto_grad", at, *args)[0]


def small_call(kernel, outs, name, at, *args):
    whole = lambda v: pl.BlockSpec(v.shape, lambda i, at, n=len(v.shape): (0,) * n)
    return pl.pallas_call(
        kernel,
        grid_spec=pltpu.PrefetchScalarGridSpec(
            num_scalar_prefetch=1,
            grid=(1,),
            in_specs=[whole(v) for v in args],
            out_specs=[whole(v) for v in outs],
        ),
        out_shape=outs,
        cost_estimate=cost(1),
        compiler_params=pltpu.CompilerParams(vmem_limit_bytes=6 * MIB),
        name=name,
    )(at, *args)


def shift(v, axis, size, d):
    return lax.ppermute(v, axis, [(i, (i + d) % size) for i in range(size)])


def exchange(v, axes):
    return lax.all_to_all(v, axes, 0, 0, tiled=False)


def shards(teacher_feat, student_feat, teacher_weight, student_weight, crop_to_image):
    ix, iz = lax.axis_index("x"), lax.axis_index("z")
    iy, ic = lax.axis_index("y"), lax.axis_index("c")
    at = jnp.stack([ix, ic, iz, iy]).astype(jnp.int32)
    group = ("x", "y", "c")
    together = lax.optimization_barrier

    tf_all = jnp.broadcast_to(teacher_feat.astype(f32)[None], (NX, TB_DEV, K))
    tf_all = exchange(tf_all, ("x",))
    rows = SB_DEV // NC
    crops = jnp.pad(crop_to_image.astype(f32).reshape(NC, rows), ((0, 6), (0, K - rows)))
    own, half = pack_pass(at, student_feat, crops)
    mine = [shift(half, "x", NX, d) for d in (1, 3, 2)]
    share = (K, COLS)
    tn, tv = norm_pass(
        at, teacher_weight, [pltpu.HBM(share, bf16), pltpu.VMEM(share, bf16)], "teacher_norm"
    )
    tf_all, tn, tv, own = together((tf_all, tn, tv, own))

    c_parts, tu = teacher_pass(tf_all, tv)
    r_parts = row_pass(exchange(c_parts, ("z",)), tu, tv)[0]
    r_parts, at_1 = together((r_parts, at))
    r_parts = exchange(r_parts, group)
    (sn,) = norm_pass(at_1, student_weight, [pltpu.HBM(share, bf16)], "student_norm")
    c_parts, sn, *mine = together((col_pass(r_parts, tu, tv), sn, *mine))
    c_parts = exchange(c_parts, ("z",))
    core = [shift(v, "c", NC, 1) for v in mine]
    c_parts, *core = together((c_parts, *core))
    r_parts, tu = together((row_pass(c_parts, tu, tv)[0], tu))
    r_parts = exchange(r_parts, group)
    mine, core = (mine[0], mine[2], mine[1]), (core[0], core[2], core[1])
    ub, ubt, ut, tuc, crops, mine = rows_pass(at, own, mine, core, tu)
    r_parts, ub, ubt, ut, tuc = together((r_parts, ub, ubt, ut, tuc))
    c_parts, ub = together((col_pass(r_parts, tu, tv), ub))
    c_parts = exchange(c_parts, ("z",))
    sums = student_pass(ub, sn)
    b, parts = row_pass(c_parts, tu, tv, sums)
    parts = exchange(parts, group)

    common = (ub, ubt, tuc, b, sn, tn)
    p0, g, coef = first_pass(at, crops, parts, *common)
    up = lambda v: shift(v, "z", NZ, 1)
    down = lambda v: shift(v, "z", NZ, -1)
    u0, d0 = up(p0[4]), down(p0[5])
    p1, g = second_pass(at, coef, g, ut, *common)
    u0, d0, g, *p1 = together((u0, d0, g, *p1))
    g = exchange(g, group)
    u1, d1 = up(p1[3]), down(p1[4])
    for k in (3, 2):
        u0, d0 = up(u0 + p0[k]), down(d0 + p0[9 - k])
        u1, d1 = up(u1 + p1[k - 1]), down(d1 + p1[8 - k])
    u0, d1 = up(u0 + p0[1]), down(d1 + p1[7])
    own, *give = merge_pass(at, p0[0], u0, d0, p1[0], u1, d1)
    got = [shift(v, "x", NX, d) for v, d in zip(give, (1, 2, 3))]
    feat_grad = feat_pass(g, mine)
    feat_grad, *got = together((feat_grad, *got))
    proto_grad = proto_pass(at, own, *got)
    feat_grad = feat_grad.T
    return (feat_grad, proto_grad)


def solution(mesh):
    split = Mesh(mesh.devices.reshape(NX, NZ, NY, NC), ("x", "z", "y", "c"))
    dp, mp = ("x", "z"), ("y", "c")
    return jax.shard_map(
        shards,
        mesh=split,
        in_specs=(P(dp, None), P(dp, None), P(None, mp), P(None, mp), P(dp)),
        out_specs=(P(dp, mp), P(dp, mp)),
        check_vma=False,
    )
```
